32 devices in a mesh: wide: 8 (over y, x, core), narrow: 4 (over z).
Axes of the slice: x: 2, y: 2, z: 4, core: 2. Of those that a mesh axis runs over, the one named last changes fastest.
Arguments:
- block_input: bfloat16 [65536, 768], P(('wide', 'narrow')), may hold values from -6 to 6
- doc_lengths: int32 [32, 4], P(('wide', 'narrow')), may hold values from 0 to 2048, as said below
- cotangent: bfloat16 [65536, 768], P(('wide', 'narrow')), may hold values from -6 to 6
- weight_query: float32 [768, 768], P(('wide', 'narrow')), may hold values from -0.21875 to 0.21875
- weight_keyval: float32 [768, 128], P(('wide', 'narrow')), may hold values from -0.21875 to 0.21875
- weight_output: float32 [768, 768], P(('wide', 'narrow')), may hold values from -0.625 to 0.625
- weight_expand: float32 [768, 3072], P(('wide', 'narrow')), may hold values from -0.21875 to 0.21875
- weight_reduce: float32 [3072, 768], P(('wide', 'narrow')), may hold values from -0.109375 to 0.109375
- momentum_query: float32 [768, 768], P(('wide', 'narrow')), may hold values from -2560 to 2560
- momentum_keyval: float32 [768, 128], P(('wide', 'narrow')), may hold values from -2560 to 2560
- momentum_output: float32 [768, 768], P(('wide', 'narrow')), may hold values from -2560 to 2560
- momentum_expand: float32 [768, 3072], P(('wide', 'narrow')), may hold values from -2560 to 2560
- momentum_reduce: float32 [3072, 768], P(('wide', 'narrow')), may hold values from -2560 to 2560
- norm_gains: float32 [2, 768], replicated, may hold values from 0.5 to 1.5
- norm_biases: float32 [2, 768], replicated, may hold values from -4 to 4
- proj_biases: float32 [5504], replicated, may hold values from -4 to 4
- adam_first: float32 [8576], replicated, may hold values from -1280 to 1280
- adam_second: float32 [8576], replicated, may hold values from 655.36 to 131072
Outputs:
- block_output: bfloat16 [65536, 768], P(('wide', 'narrow'))
- input_grad: float32 [65536, 768], P(('wide', 'narrow'))
- new_momentum_query: float32 [768, 768], P(('wide', 'narrow'))
- new_momentum_keyval: float32 [768, 128], P(('wide', 'narrow'))
- new_momentum_output: float32 [768, 768], P(('wide', 'narrow'))
- new_momentum_expand: float32 [768, 3072], P(('wide', 'narrow'))
- new_momentum_reduce: float32 [3072, 768], P(('wide', 'narrow'))
- new_weight_query: float32 [768, 768], P(('wide', 'narrow'))
- new_weight_keyval: float32 [768, 128], P(('wide', 'narrow'))
- new_weight_output: float32 [768, 768], P(('wide', 'narrow'))
- new_weight_expand: float32 [768, 3072], P(('wide', 'narrow'))
- new_weight_reduce: float32 [3072, 768], P(('wide', 'narrow'))
- vector_first: float32 [8576], replicated
- vector_second: float32 [8576], replicated
- vector_new: float32 [8576], replicated
The draws below stay inside these ranges and needn't reach their ends.
Inputs may be any that keep to these rules, and one draw needn't show every extreme that they name: `doc_lengths`: row s lists the sequence lengths of device s: nonzero ones first, each 2048, 1024 or 512, zeros for unused slots, summing to 2048.
All inputs are finite; a program needn't handle non-finite values.
Results may differ from the reference program's by a relative error of at most 0.0094.
Values may be sent and summed in bfloat16 or wider, within the bound.
No kernel may reach another device: no remote copies, remote signals or barrier semaphores. Data moves between devices by JAX's collectives and lax.ppermute only.
A program may use at most 576 MiB of HBM per device.

```python
import math
import jax
import jax.numpy as jnp
from jax import lax

D = 768
HEADS = 12
HEAD_DIM = 64
ROT = 16
FF = 3072
TOK_DEV = 2048
NS_STEPS = 5
STEP = 10
SHARDS = 32
TOKENS = 65536
QBLOCK = 512
PROJ_BIAS = 5504
VEC = 8576


def draw_doc_lengths(key, part):
    key = jax.random.fold_in(key, 11)
    pick_key, force_key = jax.random.split(key)
    patterns = jnp.array([[4, 0, 0, 0], [2, 2, 0, 0], [2, 1, 1, 0], [1, 1, 1, 1]], jnp.int32) * (TOK_DEV // 4)
    pattern_ids = jax.random.randint(pick_key, (SHARDS,), 0, 4)
    forced = jax.random.randint(force_key, (), 0, SHARDS)
    pattern_ids = pattern_ids.at[forced].set(0)
    return patterns[pattern_ids].astype(jnp.int32)


def signed_spread(key, shape, lowest, highest):
    size_key, sign_key = jax.random.split(key)
    exponent = jax.random.uniform(size_key, shape, jnp.float32, jnp.log(lowest), jnp.log(highest))
    signs = jnp.where(jax.random.bernoulli(sign_key, 0.5, shape), 1.0, -1.0)
    return (signs * jnp.exp(exponent)).astype(jnp.float32)


def draw_momentum_query(key, part):
    key = jax.random.fold_in(key, 21)
    return signed_spread(key, (D, D), 0.1, 10.0) * TOKENS ** 0.5


def draw_momentum_keyval(key, part):
    key = jax.random.fold_in(key, 22)
    return signed_spread(key, (D, 2 * HEAD_DIM), 0.1, 10.0) * TOKENS ** 0.5


def draw_momentum_output(key, part):
    key = jax.random.fold_in(key, 23)
    return signed_spread(key, (D, D), 0.1, 10.0) * TOKENS ** 0.5


def draw_momentum_expand(key, part):
    key = jax.random.fold_in(key, 24)
    return signed_spread(key, (D, FF), 0.1, 10.0) * TOKENS ** 0.5


def draw_momentum_reduce(key, part):
    key = jax.random.fold_in(key, 25)
    return signed_spread(key, (FF, D), 0.1, 10.0) * TOKENS ** 0.5


def draw_adam_first(key, part):
    key = jax.random.fold_in(key, 26)
    return signed_spread(key, (VEC,), 0.05, 5.0) * TOKENS ** 0.5


def block_levels(rng, extent, cuts, least, top_value):
    def one(position, shards_of):
        steps = jax.random.uniform(jax.random.fold_in(jax.random.fold_in(rng, 6), position), (shards_of,), jnp.float32, least / len(cuts), top_value / len(cuts))
        return jnp.repeat(jnp.exp(steps), extent[position] // shards_of).reshape((-1,) + (1,) * (len(extent) - position - 1))

    loudness = one(*cuts[0])
    for cut in cuts[1:]:
        loudness = loudness * one(*cut)
    return loudness


def scatter_about(own_key, dims, width, bound, shards=(), kind=jnp.bfloat16):
    drawn = jax.random.normal(own_key, dims, jnp.float32) * width
    if len(shards) > 0:
        drawn = block_levels(own_key, dims, shards, -0.22, 0.18) * drawn
    return jnp.clip(drawn, min=-bound, max=bound).astype(kind)


def setup_inputs(seed: int = 0) -> dict:
    seeds = jax.random.split(jax.random.key(seed), 19)
    return {
        "block_input": scatter_about(seeds[0], (TOKENS, D), 1.0, 6.0, ((0, 32),)),
        "doc_lengths": draw_doc_lengths(jax.random.fold_in(seeds[18], 71), 0),
        "cotangent": scatter_about(seeds[2], (TOKENS, D), 1.0, 6.0, ((0, 32),)),
        "weight_query": scatter_about(seeds[3], (D, D), D ** -0.5, 0.21875, ((0, 32),), jnp.float32),
        "weight_keyval": scatter_about(seeds[4], (D, 2 * HEAD_DIM), D ** -0.5, 0.21875, ((0, 32),), jnp.float32),
        "weight_output": scatter_about(seeds[5], (D, D), (D // 8) ** -0.5, 0.625, ((0, 32),), jnp.float32),
        "weight_expand": scatter_about(seeds[6], (D, FF), D ** -0.5, 0.21875, ((0, 32),), jnp.float32),
        "weight_reduce": scatter_about(seeds[7], (FF, D), FF ** -0.5, 0.109375, ((0, 32),), jnp.float32),
        "momentum_query": draw_momentum_query(jax.random.fold_in(seeds[18], 71), 0),
        "momentum_keyval": draw_momentum_keyval(jax.random.fold_in(seeds[18], 71), 0),
        "momentum_output": draw_momentum_output(jax.random.fold_in(seeds[18], 71), 0),
        "momentum_expand": draw_momentum_expand(jax.random.fold_in(seeds[18], 71), 0),
        "momentum_reduce": draw_momentum_reduce(jax.random.fold_in(seeds[18], 71), 0),
        "norm_gains": jnp.clip(1.0 + 0.1 * jax.random.normal(seeds[13], (2, D), jnp.float32), 0.5, 1.5),
        "norm_biases": scatter_about(seeds[14], (2, D), 0.3, 4.0, (), jnp.float32),
        "proj_biases": scatter_about(seeds[15], (PROJ_BIAS,), 0.3, 4.0, (), jnp.float32),
        "adam_first": draw_adam_first(jax.random.fold_in(seeds[18], 71), 0),
        "adam_second": jnp.clip(jnp.exp(jax.random.uniform(seeds[17], (VEC,), jnp.float32, math.log(655.36), math.log(131072.0))), 655.36, 131072.0),
    }


@jax.custom_vjp
def low(v):
    return lax.optimization_barrier(v.astype(jnp.bfloat16)).astype(jnp.float32)

@jax.custom_vjp
def low_back(v):
    return v

def low_keep(v):
    return (low(v), None)

def low_pass(kept, grad):
    return (grad,)

def back_keep(v):
    return (v, None)

def back_low(kept, grad):
    return (low(grad),)
low.defvjp(low_keep, low_pass)
low_back.defvjp(back_keep, back_low)
HIGHEST = lax.Precision.HIGHEST
ROPE_BASE = 10000.0
NORM_EPS = 1e-05
NS_COEFFS = (3.4445, -4.775, 2.0315)
MUON_RATE = 0.5
MUON_MOMENTUM = 0.5
ADAM_RATE = 0.3
BETA_FIRST = 0.9
BETA_SECOND = 0.95
ADAM_EPS = 1e-08

def matmul(left, right):
    return jnp.dot(left, right, precision=HIGHEST, preferred_element_type=jnp.float32)

def layer_norm(tokens, gain_row, shift_row):
    centred = tokens - lax.optimization_barrier(jnp.mean(tokens, axis=-1, keepdims=True))
    spread = lax.optimization_barrier(jnp.mean(centred * centred, axis=-1, keepdims=True))
    return centred * lax.rsqrt(spread + NORM_EPS) * gain_row + shift_row

def rotary(values, positions):
    half_rot = ROT // 2
    frequency = ROPE_BASE ** (-(2.0 * jnp.arange(half_rot, dtype=jnp.float32)) / ROT)
    angles = positions.astype(jnp.float32)[:, None] * frequency[None, :]
    cosine_table = jnp.concatenate([jnp.cos(angles), jnp.cos(angles)], axis=-1)
    sine_table = jnp.concatenate([jnp.sin(angles), jnp.sin(angles)], axis=-1)
    if values.ndim == 3:
        cosine_table = cosine_table[:, None, :]
        sine_table = sine_table[:, None, :]
    leading = values[..., :half_rot]
    trailing = values[..., half_rot:ROT]
    turned = values[..., :ROT] * cosine_table + jnp.concatenate([-trailing, leading], axis=-1) * sine_table
    return jnp.concatenate([turned, values[..., ROT:]], axis=-1)

def locate(lengths):
    doc_ends = jnp.cumsum(lengths).astype(jnp.int32)
    starts = doc_ends - lengths
    token_ids = jnp.arange(TOK_DEV, dtype=jnp.int32)
    doc_ids = lax.optimization_barrier(jnp.sum((token_ids[:, None] >= doc_ends[None, :]).astype(jnp.int32), axis=1))
    slot_ids = jnp.arange(lengths.shape[0], dtype=jnp.int32)
    doc_starts = lax.optimization_barrier(jnp.sum(jnp.where(doc_ids[:, None] == slot_ids[None, :], starts[None, :], 0), axis=1)).astype(jnp.int32)
    return (doc_ids, token_ids - doc_starts)

def attend_block(query_block, row_start, keys, values, doc_ids):
    row_ids = row_start + jnp.arange(QBLOCK, dtype=jnp.int32)
    row_docs = lax.dynamic_slice(doc_ids, (row_start,), (QBLOCK,))
    key_ids = jnp.arange(TOK_DEV, dtype=jnp.int32)
    allowed = (row_docs[:, None] == doc_ids[None, :]) & (key_ids[None, :] <= row_ids[:, None])
    scores = jnp.einsum('qhd,kd->hqk', query_block, keys, precision=HIGHEST) / math.sqrt(HEAD_DIM)
    scores = low_back(scores)
    scores = jnp.where(allowed[None], scores, -1e+30)
    row_max = lax.optimization_barrier(jnp.max(scores, axis=-1, keepdims=True))
    exp_terms = jnp.exp(scores - row_max)
    attn_probs = exp_terms / lax.optimization_barrier(jnp.sum(exp_terms, axis=-1, keepdims=True))
    return jnp.einsum('hqk,kd->qhd', low(attn_probs), values, precision=HIGHEST)

def pack_forward(tokens, lengths, rounded, gain_rows, shift_rows, biases):
    weight_query, weight_keyval, weight_output, weight_expand, weight_reduce = rounded
    bias_query = biases[:D]
    bias_keyval = biases[D:D + 2 * HEAD_DIM]
    bias_output = biases[D + 2 * HEAD_DIM:2 * D + 2 * HEAD_DIM]
    bias_expand = biases[2 * D + 2 * HEAD_DIM:2 * D + 2 * HEAD_DIM + FF]
    bias_reduce = biases[2 * D + 2 * HEAD_DIM + FF:]
    doc_ids, positions = locate(lengths)
    normed_attn = low(layer_norm(tokens, gain_rows[0], shift_rows[0]))
    normed_ffn = low(layer_norm(tokens, gain_rows[1], shift_rows[1]))
    query_pre = low_back(matmul(normed_attn, weight_query) + bias_query)
    keyval_pre = low_back(matmul(normed_attn, weight_keyval) + bias_keyval)
    queries = low(rotary(query_pre.reshape(TOK_DEV, HEADS, HEAD_DIM), positions))
    keys = low(rotary(keyval_pre[:, :HEAD_DIM], positions))
    values = low(keyval_pre[:, HEAD_DIM:])
    block_count = TOK_DEV // QBLOCK
    query_blocks = queries.reshape(block_count, QBLOCK, HEADS, HEAD_DIM)
    block_starts = jnp.arange(block_count, dtype=jnp.int32) * QBLOCK

    def one_block(packed):
        return attend_block(packed[0], packed[1], keys, values, doc_ids)
    mixed = lax.map(jax.checkpoint(one_block), (query_blocks, block_starts)).reshape(TOK_DEV, D)
    mixed = low(low_back(mixed))
    attn_branch = matmul(mixed, weight_output) + bias_output
    expand_pre = low_back(matmul(normed_ffn, weight_expand) + bias_expand)
    activated = low(jax.nn.gelu(expand_pre, approximate=False))
    ffn_branch = matmul(activated, weight_reduce) + bias_reduce
    return tokens + attn_branch + ffn_branch

def newton_schulz(matrix):
    is_tall = matrix.shape[0] > matrix.shape[1]
    iterate = matrix.T if is_tall else matrix
    iterate = iterate / (jnp.sqrt(jnp.sum(iterate * iterate)) + 1e-07)
    for sweep in range(NS_STEPS):
        gram_matrix = matmul(iterate, iterate.T)
        polynomial = NS_COEFFS[1] * gram_matrix + NS_COEFFS[2] * matmul(gram_matrix, gram_matrix)
        iterate = NS_COEFFS[0] * iterate + matmul(polynomial, iterate)
    return iterate.T if is_tall else iterate

def reference(block_input, doc_lengths, cotangent, weight_query, weight_keyval, weight_output, weight_expand, weight_reduce, momentum_query, momentum_keyval, momentum_output, momentum_expand, momentum_reduce, norm_gains, norm_biases, proj_biases, adam_first, adam_second):
    masters = (weight_query, weight_keyval, weight_output, weight_expand, weight_reduce)
    momenta = (momentum_query, momentum_keyval, momentum_output, momentum_expand, momentum_reduce)
    rounded = tuple((lax.optimization_barrier(master.astype(jnp.bfloat16)).astype(jnp.float32) for master in masters))
    tokens = block_input.astype(jnp.float32).reshape(SHARDS, TOK_DEV, D)

    def whole_layer(tokens, rounded, gain_rows, shift_rows, biases):

        def one_pack(packed):
            return pack_forward(packed[0], packed[1], rounded, gain_rows, shift_rows, biases)
        return lax.map(jax.checkpoint(one_pack), (tokens, doc_lengths))
    outputs, pullback = jax.vjp(whole_layer, tokens, rounded, norm_gains, norm_biases, proj_biases)
    grad_tokens, grad_weights, grad_gains, grad_shifts, grad_biases = pullback(cotangent.astype(jnp.float32).reshape(SHARDS, TOK_DEV, D))
    block_output = outputs.reshape(TOKENS, D).astype(jnp.bfloat16)
    input_grad = grad_tokens.reshape(TOKENS, D)
    new_momenta = []
    new_weights = []
    for master, momentum, gradient in zip(masters, momenta, grad_weights):
        fresh = MUON_MOMENTUM * momentum + gradient
        orthogonal = newton_schulz(fresh)
        factor = math.sqrt(max(1.0, master.shape[0] / master.shape[1]))
        new_momenta.append(fresh)
        new_weights.append(master - MUON_RATE * factor * orthogonal)
    vector_grad = jnp.concatenate([grad_gains.reshape(-1), grad_shifts.reshape(-1), grad_biases])
    params = jnp.concatenate([norm_gains.reshape(-1), norm_biases.reshape(-1), proj_biases])
    vector_first = BETA_FIRST * adam_first + (1.0 - BETA_FIRST) * vector_grad
    vector_second = BETA_SECOND * adam_second + (1.0 - BETA_SECOND) * vector_grad * vector_grad
    corrected_first = vector_first / (1.0 - BETA_FIRST ** STEP)
    corrected_second = vector_second / (1.0 - BETA_SECOND ** STEP)
    vector_new = params - ADAM_RATE * corrected_first / (jnp.sqrt(corrected_second) + ADAM_EPS)
    return (block_output, input_grad, new_momenta[0], new_momenta[1], new_momenta[2], new_momenta[3], new_momenta[4], new_weights[0], new_weights[1], new_weights[2], new_weights[3], new_weights[4], vector_first, vector_second, vector_new)
```

```python
from functools import partial
import math

import jax
import jax.numpy as jnp
from jax import lax
from jax.experimental import pallas as pl
from jax.experimental.pallas import tpu as pltpu
from jax.sharding import Mesh, PartitionSpec as P

D = 768
HEADS = 12
HEAD_DIM = 64
ROT = 16
FF = 3072
TOK = 2048
NS_STEPS = 5
STEP = 10
QB = 512
HALF = 256
NH = 4
GROUP = NH * HEAD_DIM
FC = 768
BF = jnp.bfloat16
F32 = jnp.float32
LOG2E = 1.4426950408889634
MIB = 1024 * 1024


def dot(a, b):
    return jnp.dot(a, b, preferred_element_type=F32)


def dot_nt(a, b):
    return lax.dot_general(a, b, (((1,), (1,)), ((), ())), preferred_element_type=F32)


def dot_tn(a, b):
    return lax.dot_general(a, b, (((0,), (0,)), ((), ())), preferred_element_type=F32)


def attention_kernel(opening, closing, *refs):
    first_ref, q_ref, do_ref, cos_ref, sin_ref, kv_ref = refs[:6]
    start_ref = None if opening else refs[9]
    refs = refs[7:] if opening else refs[10:]
    mix_ref, dq_ref, dkv_ref = refs[:3]
    refs = refs[3:]
    if closing:
        gkv_ref = refs[0]
        refs = refs[1:]
    (k_ref, kt_ref, vx_ref, vt_ref, qz_ref, e_even, e_odd, acc_ref, m_ref, mh_ref, rhs_ref, dl_ref,
     dqa_ref) = refs
    e_ref = (e_even, e_odd)
    hg = pl.program_id(0)
    qi = pl.program_id(1)
    first = first_ref[qi]
    diag = pl.multiple_of(qi * QB, QB)
    here = pl.ds(diag, QB)

    @pl.when((hg == 0) & (qi == 0))
    def _():
        dkv_ref[...] = jnp.zeros_like(dkv_ref) if opening else start_ref[...]
        filler = jnp.where(lax.broadcasted_iota(jnp.int32, (HEAD_DIM, QB), 0) < 2, 1.0, 0.0)
        for j in range(TOK // QB):
            cols = slice(j * QB, (j + 1) * QB)
            c, s = cos_ref[:, cols], sin_ref[:, cols]
            u = kv_ref[0:HEAD_DIM, cols]
            v = kv_ref[HEAD_DIM:, cols]
            k = jnp.concatenate(
                [u[0:8] * c - u[8:16] * s, u[8:16] * c + u[0:8] * s, u[16:]], axis=0
            )
            kt_ref[:, cols] = k.astype(BF)
            vt_ref[0:HEAD_DIM, cols] = v.astype(BF)
            vt_ref[HEAD_DIM:, cols] = jnp.ones((16, QB), BF)
            both = jnp.concatenate([k, v], axis=0).T
            k_ref[cols, :] = both[:, 0:HEAD_DIM].astype(BF)
            vx_ref[cols, :] = jnp.concatenate([filler, v], axis=0).T.astype(BF)

    cos = cos_ref[:, here]
    sin = sin_ref[:, here]
    scale = LOG2E / math.sqrt(HEAD_DIM)
    for h in range(NH):
        u = q_ref[h * HEAD_DIM : (h + 1) * HEAD_DIM, :]
        a, b = u[0:8], u[8:16]
        turned = jnp.concatenate([a * cos - b * sin, b * cos + a * sin, u[16:]], axis=0)
        qz_ref[h, 0:HEAD_DIM, :] = (turned * scale).astype(BF)
        qz_ref[h, HEAD_DIM:, :] = jnp.zeros((HEAD_DIM, QB), BF)

    def edge_mask(c):
        shape = ((c + 1) * HALF, HALF)
        keys_in = lax.broadcasted_iota(jnp.int32, shape, 0)
        return keys_in <= lax.broadcasted_iota(jnp.int32, shape, 1) + c * HALF

    row16 = lax.broadcasted_iota(jnp.int32, (HEAD_DIM, QB), 0)
    zeros = jnp.zeros((HEAD_DIM, QB), BF)

    def edges(h, c):
        q = qz_ref[h, 0:HEAD_DIM, c * HALF : (c + 1) * HALF]
        s = dot(k_ref[pl.ds(diag, (c + 1) * HALF), :], q)
        return jnp.where(edge_mask(c), s, -1e30)

    def forward_diagonal(h, s, c):
        cols = slice(c * HALF, (c + 1) * HALF)
        rows = pl.ds(diag, (c + 1) * HALF)
        m = jnp.max(s, axis=0, keepdims=True)
        e = jnp.exp2(s - m).astype(BF)
        e_ref[h % 2][rows, cols] = e
        acc_ref[h, :, cols] = dot(vt_ref[:, rows], e)
        m_ref[h, :, cols] = m

    def forward(h, s, off, j):
        m_old = m_ref[h]
        m = jnp.maximum(m_old, jnp.max(s, axis=0, keepdims=True))
        e = jnp.exp2(s - m).astype(BF)
        e_ref[h % 2][pl.ds(off, QB), :] = e
        acc_ref[h] = acc_ref[h] * jnp.exp2(m_old - m) + dot(vt_ref[:, pl.ds(off, QB)], e)
        m_ref[h] = m
        mh_ref[j, h] = m

    def between(h):
        rows = slice(h * HEAD_DIM, (h + 1) * HEAD_DIM)
        inv = 1.0 / acc_ref[h, HEAD_DIM : HEAD_DIM + 1, :]
        mixed = acc_ref[h, 0:HEAD_DIM, :] * inv
        mix_ref[rows, :] = mixed.astype(BF)
        do = do_ref[rows, :].astype(F32)
        delta = jnp.sum(do * mixed, axis=0, keepdims=True)
        rhs_ref[h] = do * inv
        dl_ref[h] = -(delta * inv)

    def scaled(h, j):
        r = jnp.exp2(mh_ref[j, h] - m_ref[h])
        dop = (rhs_ref[h] * r).astype(BF)
        dl = dl_ref[h] * r
        hi = dl.astype(BF).astype(F32)
        lo = dl - hi
        head = jnp.where(row16 == 0, hi, jnp.where(row16 == 1, lo, 0.0)).astype(BF)
        return jnp.concatenate([head, dop], axis=0), jnp.concatenate([zeros, dop], axis=0)

    def backward_diagonal(h, rhs, rz, c):
        cols = slice(c * HALF, (c + 1) * HALF)
        rows = pl.ds(diag, (c + 1) * HALF)
        x = dot(vx_ref[rows, :], rhs[:, cols])
        e = e_ref[h % 2][rows, cols]
        ds = e * x.astype(BF)
        dqa_ref[h, :, cols] = dot(kt_ref[:, rows], ds)
        dkv_ref[rows, :] += dot_nt(ds, qz_ref[h, :, cols]) + dot_nt(e, rz[:, cols])

    def backward(h, x, rz, off):
        e = e_ref[h % 2][pl.ds(off, QB), :]
        ds = e * x.astype(BF)
        dqa_ref[h] += dot(kt_ref[:, pl.ds(off, QB)], ds)
        dkv_ref[pl.ds(off, QB), :] += dot_nt(ds, qz_ref[h]) + dot_nt(e, rz)

    for h in range(NH + 1):
        ahead, behind = h < NH, h > 0
        if behind:
            rhs, rz = scaled(h - 1, qi)
        for c in range(2):
            if ahead:
                parts = edges(h, c)
            if behind:
                backward_diagonal(h - 1, rhs, rz, c)
            if ahead:
                forward_diagonal(h, parts, c)
        if ahead:
            mh_ref[qi, h] = m_ref[h]

        def block(j, carry, h=h, ahead=ahead, behind=behind):
            off = pl.multiple_of(j * QB, QB)
            if ahead:
                s = dot(k_ref[pl.ds(off, QB), :], qz_ref[h, 0:HEAD_DIM, :])
            if behind:
                rhs, rz = scaled(h - 1, j)
                x = dot(vx_ref[pl.ds(off, QB), :], rhs)
                backward(h - 1, x, rz, off)
            if ahead:
                forward(h, s, off, j)
            return carry

        lax.fori_loop(first, qi, block, 0)
        if ahead:
            between(h)

    for h in range(NH):
        u = dqa_ref[h] * (1.0 / math.sqrt(HEAD_DIM))
        a, b = u[0:8], u[8:16]
        turned = jnp.concatenate([a * cos + b * sin, b * cos - a * sin, u[16:]], axis=0)
        dq_ref[h * HEAD_DIM : (h + 1) * HEAD_DIM, :] = turned.astype(BF)

    if closing:

        @pl.when((hg == pl.num_programs(0) - 1) & (qi == pl.num_programs(1) - 1))
        def _():
            for j in range(TOK // QB):
                cols = slice(j * QB, (j + 1) * QB)
                c, s = cos_ref[:, cols], sin_ref[:, cols]
                t = dkv_ref[cols, :].T
                u = t[0:HEAD_DIM] * math.log(2.0)
                k = jnp.concatenate(
                    [u[0:8] * c + u[8:16] * s, u[8:16] * c - u[0:8] * s, u[16:], t[HEAD_DIM:]], axis=0
                )
                gkv_ref[:, cols] = k.astype(BF)


def attention(first, qkv_t, grad_mixed, cos, sin, after, group_lo, groups, so_far):
    blocks = TOK // QB
    opening, closing = so_far is None, (group_lo + groups) * GROUP == D
    group_block = pl.BlockSpec((GROUP, QB), lambda g, i, f: (group_lo + g, i))

    def whole(shape, row=0):
        return pl.BlockSpec(shape, lambda g, i, f: (row, 0))

    anywhere = pl.BlockSpec(memory_space=pl.ANY)
    in_specs = [
        group_block, group_block, whole((8, TOK)), whole((8, TOK)), whole((128, TOK), D // 128), anywhere,
    ]
    operands = [first, qkv_t, grad_mixed, cos, sin, qkv_t, after]
    aliases = {}
    if not opening:
        in_specs += [anywhere, anywhere, whole((TOK, 128))]
        operands += list(so_far)
        aliases = {7: 0, 8: 1}
    out_specs = [group_block, group_block, whole((TOK, 128))]
    out_shape = [
        jax.ShapeDtypeStruct((D, TOK), BF),
        jax.ShapeDtypeStruct((D, TOK), BF),
        jax.ShapeDtypeStruct((TOK, 128), F32),
    ]
    if closing:
        out_specs.append(whole((128, TOK)))
        out_shape.append(jax.ShapeDtypeStruct((128, TOK), BF))
    return pl.pallas_call(
        partial(attention_kernel, opening, closing),
        grid_spec=pltpu.PrefetchScalarGridSpec(
            num_scalar_prefetch=1,
            grid=(groups, blocks),
            in_specs=in_specs,
            out_specs=out_specs,
            scratch_shapes=[
                pltpu.VMEM((TOK, HEAD_DIM), BF),
                pltpu.VMEM((HEAD_DIM, TOK), BF),
                pltpu.VMEM((TOK, 128), BF),
                pltpu.VMEM((80, TOK), BF),
                pltpu.VMEM((NH, 128, QB), BF),
                pltpu.VMEM((TOK, QB), BF),
                pltpu.VMEM((TOK, QB), BF),
                pltpu.VMEM((NH, 80, QB), F32),
                pltpu.VMEM((NH, 1, QB), F32),
                pltpu.VMEM((blocks, NH, 1, QB), F32),
                pltpu.VMEM((NH, HEAD_DIM, QB), F32),
                pltpu.VMEM((NH, 1, QB), F32),
                pltpu.VMEM((NH, HEAD_DIM, QB), F32),
            ],
        ),
        out_shape=out_shape,
        input_output_aliases=aliases,
        compiler_params=pltpu.CompilerParams(
            dimension_semantics=("arbitrary", "arbitrary"), vmem_limit_bytes=48 * MIB
        ),
        cost_estimate=pl.CostEstimate(
            flops=groups * NH * 6 * 2 * TOK * TOK // 2 * 256,
            bytes_accessed=groups * GROUP * TOK * 10,
            transcendentals=groups * NH * TOK * TOK // 2,
        ),
        name="attention",
    )(*operands)


ERF = (0.254829592, -0.284496736, 1.421413741, -1.453152027, 1.061405429)


def gelu_pair(x):
    e = jnp.exp2(x * x * (-0.5 * LOG2E))
    den = 1.0 + (0.3275911 / math.sqrt(2.0)) * jnp.abs(x)
    t = 1.0 / den
    p = ERF[4]
    for c in (ERF[3], ERF[2], ERF[1], ERF[0]):
        p = p * t + c
    tail = (0.5 * p) * (t * e)
    phi = jnp.where(x >= 0.0, 1.0 - tail, tail)
    return phi, phi + x * (e * (1.0 / math.sqrt(2.0 * math.pi)))


def ffn_kernel(
    x_ref, xt_ref, g_ref, gt_ref, up_ref, down_ref, bias_ref, _,
    y_ref, dx_ref, dup_ref, ddown_ref, db_ref,
    pre_ref, grad_ref, act_ref, de_ref, dn_ref,
):
    tile = TOK // 2
    part = 256

    @pl.when(pl.program_id(0) == 0)
    def _():
        y_ref[...] = jnp.zeros_like(y_ref)
        dx_ref[...] = jnp.zeros_like(dx_ref)

    fold = FC // 4
    for q in range(4):
        dn_ref[q * fold : (q + 1) * fold, :] = down_ref[:, q * D : (q + 1) * D]

    for t in range(TOK // tile):
        rows = slice(t * tile, (t + 1) * tile)
        pre_ref[rows, :] = dot(x_ref[rows, :], up_ref[...])
        grad_ref[rows, :] = dot_nt(g_ref[rows, :], dn_ref[...])
    db = jnp.zeros((1, FC), F32)
    for t in range(TOK // tile):
        rows = slice(t * tile, (t + 1) * tile)
        for lo in range(t * tile, (t + 1) * tile, part):
            some = slice(lo, lo + part)
            pre = pre_ref[some, :] + bias_ref[...]
            phi, slope = gelu_pair(pre)
            act_ref[some, :] = (pre * phi).astype(BF)
            d = slope * grad_ref[some, :]
            db = db + jnp.sum(d, axis=0, keepdims=True)
            de_ref[some, :] = d.astype(BF)
        y_ref[rows, :] += dot(act_ref[rows, :], dn_ref[...])
        dx_ref[rows, :] += dot_nt(de_ref[rows, :], up_ref[...])
    db_ref[...] = db
    dup_ref[...] = dot(xt_ref[...], de_ref[...]).astype(BF)
    dd = dot(gt_ref[...], act_ref[...]).T.astype(BF)
    for q in range(4):
        ddown_ref[:, q * D : (q + 1) * D] = dd[q * fold : (q + 1) * fold, :]


def ffn(x, xt, g, gt, weights, bias, after):
    once = pl.Buffered(1)

    def whole(shape):
        return pl.BlockSpec(shape, lambda c: (0, 0), pipeline_mode=once)

    return pl.pallas_call(
        ffn_kernel,
        grid=(FF // FC,),
        in_specs=[
            whole((TOK, D)), whole((D, TOK)), whole((TOK, D)), whole((D, TOK)),
            pl.BlockSpec((D, FC), lambda c: (0, c)),
            pl.BlockSpec((FC // 4, FF), lambda c: (c, 1)),
            pl.BlockSpec((1, FC), lambda c: (0, c)),
            pl.BlockSpec(memory_space=pl.ANY),
        ],
        out_specs=[
            whole((TOK, D)), whole((TOK, D)),
            pl.BlockSpec((D, FC), lambda c: (0, c)),
            pl.BlockSpec((FC // 4, FF), lambda c: (c, 0)),
            pl.BlockSpec((1, FC), lambda c: (0, c)),
        ],
        scratch_shapes=[pltpu.VMEM((TOK, FC), F32)] * 2
        + [pltpu.VMEM((TOK, FC), BF)] * 2 + [pltpu.VMEM((FC, D), BF)],
        out_shape=[
            jax.ShapeDtypeStruct((TOK, D), F32),
            jax.ShapeDtypeStruct((TOK, D), F32),
            jax.ShapeDtypeStruct((D, FF), BF),
            jax.ShapeDtypeStruct((D, FF), BF),
            jax.ShapeDtypeStruct((1, FF), F32),
        ],
        compiler_params=pltpu.CompilerParams(
            dimension_semantics=("arbitrary",), vmem_limit_bytes=58 * MIB
        ),
        cost_estimate=pl.CostEstimate(
            flops=12 * TOK * D * FF, bytes_accessed=44 * MIB, transcendentals=2 * TOK * FF
        ),
        name="ffn",
    )(x, xt, g, gt, weights, weights, bias, after)


ROPE_BASE = 10000.0
NORM_EPS = 1e-05
NS_A, NS_B, NS_C = 3.4445, -4.775, 2.0315
MUON_RATE = 0.5
MUON_MOMENTUM = 0.5
ADAM_RATE = 0.3
BETA_FIRST = 0.9
BETA_SECOND = 0.95
ADAM_EPS = 1e-08
QKV = D + 2 * HEAD_DIM


def prepare_kernel(x_ref, g_ref, gain_ref, shift_ref, na_t_ref, nf_ref, nf_t_ref, g_t_ref):
    x = x_ref[...].astype(F32)
    centred = x - jnp.mean(x, axis=-1, keepdims=True)
    hat = centred * lax.rsqrt(jnp.mean(centred * centred, axis=-1, keepdims=True) + NORM_EPS)
    na_t_ref[...] = (hat * gain_ref[0:1, :] + shift_ref[0:1, :]).T.astype(BF)
    nf = hat * gain_ref[1:2, :] + shift_ref[1:2, :]
    nf_ref[...] = nf.astype(BF)
    nf_t_ref[...] = nf.T.astype(BF)
    g_t_ref[...] = g_ref[...].astype(F32).T.astype(BF)


def prepare(x, g, gains, shifts):
    block = 512
    rows = pl.BlockSpec((block, D), lambda i: (i, 0))
    cols = pl.BlockSpec((D, block), lambda i: (0, i))
    fixed = pl.BlockSpec((2, D), lambda i: (0, 0))
    turned = jax.ShapeDtypeStruct((D, TOK), BF)
    return pl.pallas_call(
        prepare_kernel,
        grid=(TOK // block,),
        in_specs=[rows, rows, fixed, fixed],
        out_specs=[cols, rows, cols, cols],
        out_shape=[turned, jax.ShapeDtypeStruct((TOK, D), BF), turned, turned],
        compiler_params=pltpu.CompilerParams(
            dimension_semantics=("arbitrary",), vmem_limit_bytes=48 * MIB
        ),
        cost_estimate=pl.CostEstimate(
            flops=20 * TOK * D, bytes_accessed=12 * TOK * D, transcendentals=TOK
        ),
        name="prepare",
    )(x, g, gains, shifts)


def grads_kernel(g_ref, mix_ref, gq_ref, gkv_ref, nt_ref, dqkv_ref, dout_ref, bsum_ref, qkv_acc, out_acc):
    i = pl.program_id(0)
    gq = gq_ref[...]
    gkv = gkv_ref[...]
    nt = nt_ref[...]

    @pl.when(i == 0)
    def _():
        qkv_acc[...] = jnp.zeros_like(qkv_acc)
        out_acc[...] = jnp.zeros_like(out_acc)
        bsum_ref[...] = jnp.zeros_like(bsum_ref)

    qkv_acc[:, 0:D] += dot_nt(nt, gq)
    qkv_acc[:, D:] += dot_nt(nt, gkv)
    out_acc[...] += dot(mix_ref[...], g_ref[...])
    ones = jnp.ones((8, gq.shape[1]), BF)
    bsum_ref[:, 0:D] += dot_nt(ones, gq)
    bsum_ref[:, D:] += dot_nt(ones, gkv)

    @pl.when(i == pl.num_programs(0) - 1)
    def _():
        dqkv_ref[...] = qkv_acc[...].astype(BF)
        dout_ref[...] = out_acc[...].astype(BF)


def grads(g, mix, gq, gkv, nt):
    block = 1024
    cols = pl.BlockSpec((D, block), lambda i: (0, i))

    def fixed(shape):
        return pl.BlockSpec(shape, lambda i: (0, 0))

    return pl.pallas_call(
        grads_kernel,
        grid=(TOK // block,),
        in_specs=[
            pl.BlockSpec((block, D), lambda i: (i, 0)), cols, cols,
            pl.BlockSpec((128, block), lambda i: (0, i)), cols,
        ],
        out_specs=[fixed((D, QKV)), fixed((D, D)), fixed((8, QKV))],
        scratch_shapes=[pltpu.VMEM((D, QKV), F32), pltpu.VMEM((D, D), F32)],
        out_shape=[
            jax.ShapeDtypeStruct((D, QKV), BF), jax.ShapeDtypeStruct((D, D), BF),
            jax.ShapeDtypeStruct((8, QKV), F32),
        ],
        compiler_params=pltpu.CompilerParams(
            dimension_semantics=("arbitrary",), vmem_limit_bytes=48 * MIB
        ),
        cost_estimate=pl.CostEstimate(
            flops=2 * TOK * D * (QKV + D), bytes_accessed=16 * MIB, transcendentals=0
        ),
        name="grads",
    )(g, mix, gq, gkv, nt)


def final_kernel(
    x_ref, g_ref, y_ref, df_ref, mix_ref, gq_ref, gkv_ref, wt_ref, wo_ref, gain_ref, bias_ref,
    out_ref, ig_ref, sums_ref,
):
    i = pl.program_id(0)
    x = x_ref[...].astype(F32)
    gf = g_ref[...].astype(F32)

    @pl.when(i == 0)
    def _():
        sums_ref[...] = jnp.zeros_like(sums_ref)

    da = dot_tn(gq_ref[...], wt_ref[0:D, :]) + dot_tn(gkv_ref[...], wt_ref[D:, :])
    out_ref[...] = (x + (dot_tn(mix_ref[...], wo_ref[...]) + y_ref[...] + bias_ref[...])).astype(BF)
    mean = jnp.mean(x, axis=-1, keepdims=True)
    centred = x - mean
    rstd = lax.rsqrt(jnp.mean(centred * centred, axis=-1, keepdims=True) + NORM_EPS)
    hat = centred * rstd
    df = df_ref[...]
    d_hat = da * gain_ref[0:1, :] + df * gain_ref[1:2, :]
    m1 = jnp.mean(d_hat, axis=-1, keepdims=True)
    m2 = jnp.mean(d_hat * hat, axis=-1, keepdims=True)
    ig_ref[...] = gf + rstd * (d_hat - m1 - hat * m2)
    for r, v in enumerate((da * hat, df * hat, da, df, gf)):
        sums_ref[r : r + 1, :] += jnp.sum(v, axis=0, keepdims=True)


def final(x, g, y, d_ffn, mix, gq, gkv, wt, wo, gains, bias):
    block = 512

    def rows(i):
        return (i, 0)

    def cols(i):
        return (0, i)

    def fixed(i):
        return (0, 0)

    return pl.pallas_call(
        final_kernel,
        grid=(TOK // block,),
        in_specs=[
            pl.BlockSpec((block, D), rows), pl.BlockSpec((block, D), rows),
            pl.BlockSpec((block, D), rows), pl.BlockSpec((block, D), rows),
            pl.BlockSpec((D, block), cols), pl.BlockSpec((D, block), cols),
            pl.BlockSpec((128, block), cols),
            pl.BlockSpec((QKV, D), fixed), pl.BlockSpec((D, D), fixed),
            pl.BlockSpec((2, D), fixed), pl.BlockSpec((1, D), fixed),
        ],
        out_specs=[
            pl.BlockSpec((block, D), rows), pl.BlockSpec((block, D), rows), pl.BlockSpec((8, D), fixed),
        ],
        out_shape=[
            jax.ShapeDtypeStruct((TOK, D), BF), jax.ShapeDtypeStruct((TOK, D), F32),
            jax.ShapeDtypeStruct((8, D), F32),
        ],
        compiler_params=pltpu.CompilerParams(
            dimension_semantics=("arbitrary",), vmem_limit_bytes=48 * MIB
        ),
        cost_estimate=pl.CostEstimate(
            flops=2 * TOK * D * (QKV + D), bytes_accessed=36 * MIB, transcendentals=TOK
        ),
        name="closing",
    )(x, g, y, d_ffn, mix, gq, gkv, wt, wo, gains, bias)


def eye_block(rows, n, row_lo):
    r = lax.broadcasted_iota(jnp.int32, (rows, n), 0) + row_lo
    return r == lax.broadcasted_iota(jnp.int32, (rows, n), 1)


def diagonal_sum(ref, n, blk):
    total = 0.0
    for r in range(0, n, blk):
        total += jnp.sum(jnp.where(eye_block(blk, blk, 0), ref[r : r + blk, r : r + blk], 0.0))
    return total


def shift_diagonal(ref, low_ref, level, n, blk):
    for r in range(0, n, blk):
        ref[r : r + blk, r : r + blk] -= jnp.where(eye_block(blk, blk, 0), level, 0.0)
        low_ref[r : r + blk, :] = ref[r : r + blk, :].astype(BF)


def recentre(ref, low_ref, n, blk):
    level = diagonal_sum(ref, n, blk) / n
    shift_diagonal(ref, low_ref, level, n, blk)
    return level


def gram_sweep(level, q0, n, blk, a, al, s, sl, t, tl, u, ul, first=False, last=False):
    p0 = NS_A + NS_B * level + NS_C * level * level
    s[...] = (NS_B + 2.0 * NS_C * level) * a[...] + NS_C * dot(al[...], al[...])
    sl[...] = s[...].astype(BF)
    if first:
        u[...] = s[...]
        q0 = p0
    else:
        u[...] = p0 * u[...] + q0 * s[...] + dot(sl[...], ul[...])
        q0 = p0 * q0
    q0 = q0 + recentre(u, ul, n, blk)
    if last:
        return level, q0
    t[...] = p0 * a[...] + level * s[...] + dot(sl[...], al[...])
    t0 = p0 * level + recentre(t, tl, n, blk)
    a[...] = p0 * t[...] + t0 * s[...] + dot(sl[...], tl[...])
    return p0 * t0 + recentre(a, al, n, blk), q0


def wide_kernel(down_ref, m_ref, u_ref, q_ref, a, al, s, sl, t, tl, u, ul):
    blk = 256

    @pl.when(down_ref[0] == 0)
    def _():
        a[...] = dot_nt(m_ref[...], m_ref[...])

    @pl.when(down_ref[0] != 0)
    def _():
        for q in range(4):
            part = m_ref[:, q * D : (q + 1) * D]
            if q == 0:
                a[...] = dot_tn(part, part)
            else:
                a[...] += dot_tn(part, part)

    inverse = 1.0 / (jnp.sqrt(jnp.full((1, D), diagonal_sum(a, D, blk))) + 1e-07)
    a[...] = a[...] * (inverse * inverse)
    level = recentre(a, al, D, blk)
    state = (a, al, s, sl, t, tl, u, ul)

    def sweep(k, carry):
        return gram_sweep(carry[0], carry[1], D, blk, *state)

    carry = gram_sweep(level, None, D, blk, *state, first=True)
    carry = lax.fori_loop(1, NS_STEPS - 1, sweep, carry)
    _, q0 = gram_sweep(carry[0], carry[1], D, blk, *state, last=True)
    u_ref[...] = (u[...] * inverse).astype(BF)
    q_ref[...] = q0 * inverse


def wide_ns(down, m):
    big, low = pltpu.VMEM((D, D), F32), pltpu.VMEM((D, D), BF)

    def fixed(i, d):
        return (0, 0)

    return pl.pallas_call(
        wide_kernel,
        grid_spec=pltpu.PrefetchScalarGridSpec(
            num_scalar_prefetch=1,
            grid=(1,),
            in_specs=[pl.BlockSpec((D, FF), lambda i, d: (0, d[0]), pipeline_mode=pl.Buffered(1))],
            out_specs=[pl.BlockSpec((D, D), fixed), pl.BlockSpec((1, D), fixed)],
            scratch_shapes=[big, low] * 4,
        ),
        out_shape=[jax.ShapeDtypeStruct((D, D), BF), jax.ShapeDtypeStruct((1, D), F32)],
        compiler_params=pltpu.CompilerParams(vmem_limit_bytes=48 * MIB),
        cost_estimate=pl.CostEstimate(flops=2 * 24 * D**3, bytes_accessed=6 * MIB, transcendentals=D),
        name="wide_ns",
    )(down, m)


def square_kernel(m_ref, kv_ref, o_ref, okv_ref, x, xl, a, al, sl, *small):
    blk = 256
    n = 2 * HEAD_DIM
    m = m_ref[...].astype(F32)
    x[...] = m / (jnp.sqrt(jnp.full((1, D), jnp.sum(m * m))) + 1e-07)
    sa, sal, ss, ssl, st, stl, su, sul = small
    kv = kv_ref[...]
    sa[...] = dot_tn(kv, kv)
    inverse = 1.0 / (jnp.sqrt(jnp.full((1, n), diagonal_sum(sa, n, n))) + 1e-07)
    sa[...] = sa[...] * (inverse * inverse)
    su[...] = jnp.zeros_like(su)
    sul[...] = jnp.zeros_like(sul)
    level = recentre(sa, sal, n, n)

    def sweep(k, carry):
        xl[...] = x[...].astype(BF)
        a[...] = dot_nt(xl[...], xl[...])
        lev = recentre(a, al, D, blk)
        p0 = NS_A + NS_B * lev + NS_C * lev * lev
        small_next = gram_sweep(carry[0], carry[1], n, n, sa, sal, ss, ssl, st, stl, su, sul)
        sl[...] = ((NS_B + 2.0 * NS_C * lev) * a[...] + NS_C * dot(al[...], al[...])).astype(BF)
        x[...] = p0 * x[...] + dot(sl[...], xl[...])
        return small_next

    _, q0 = lax.fori_loop(0, NS_STEPS, sweep, (level, jnp.float32(1.0)))
    o_ref[...] = x[...]
    okv_ref[...] = (q0 * kv.astype(F32) + dot(kv, sul[...])) * inverse


def square_ns(m, kv):
    big, low = pltpu.VMEM((D, D), F32), pltpu.VMEM((D, D), BF)
    n = 2 * HEAD_DIM
    return pl.pallas_call(
        square_kernel,
        in_specs=[pl.BlockSpec(memory_space=pltpu.VMEM)] * 2,
        out_specs=[pl.BlockSpec(memory_space=pltpu.VMEM)] * 2,
        scratch_shapes=[big, low, big, low, low]
        + [pltpu.VMEM((n, n), F32), pltpu.VMEM((n, n), BF)] * 4,
        out_shape=[jax.ShapeDtypeStruct((D, D), F32), jax.ShapeDtypeStruct((D, n), F32)],
        compiler_params=pltpu.CompilerParams(vmem_limit_bytes=48 * MIB),
        cost_estimate=pl.CostEstimate(flops=2 * 17 * D**3, bytes_accessed=6 * MIB, transcendentals=D),
        name="square_ns",
    )(m, kv)


def swap(x, axis, bit):
    return lax.ppermute(x, axis, [(i, i ^ bit) for i in range(lax.axis_size(axis))])


def bits_of(size):
    return [1 << b for b in range(size.bit_length() - 1)]


class Grid:
    def __init__(self):
        chip, narrow = bits_of(lax.axis_size("chip")), bits_of(lax.axis_size("narrow"))
        self.axes = [("chip", b) for b in reversed(chip)] + [("core", 1)]
        self.axes += [("narrow", b) for b in reversed(narrow)]
        self.chip = list(range(len(chip)))
        self.core = len(chip)
        self.narrow = list(range(len(chip) + 1, len(self.axes)))

    def bit(self, place):
        axis, bit = self.axes[place]
        return (lax.axis_index(axis) // bit) % 2

    def swap(self, x, place):
        return swap(x, *self.axes[place])

    def gather(self, x, order):
        x = x.reshape((1,) * len(self.axes) + x.shape)
        for place in order:
            other = self.swap(x, place)
            up = self.bit(place) == 1
            x = jnp.concatenate([jnp.where(up, other, x), jnp.where(up, x, other)], axis=place)
        return x.reshape((-1,) + x.shape[len(self.axes) + 1 :])

    def scatter(self, x, order):
        x = x.reshape((2,) * len(self.axes) + (-1,) + x.shape[1:])
        passed = []
        for place in order:
            bit = self.bit(place)
            away = lax.dynamic_index_in_dim(x, 1 - bit, place, keepdims=True).astype(BF)
            keep = lax.dynamic_index_in_dim(x, bit, place, keepdims=True).astype(F32)
            x = keep + self.swap(away, place).astype(F32)
            passed.append(x)
        return x.reshape((-1,) + x.shape[len(self.axes) + 1 :]), passed


def locate(lengths):
    ends = jnp.cumsum(lengths)
    token_ids = jnp.arange(TOK, dtype=jnp.int32)
    starts = jnp.max(jnp.where(ends[None, :] <= token_ids[:, None], ends[None, :], 0), axis=1)
    return starts, token_ids - starts


def up_columns(x):
    return x.reshape(x.shape[0], FF // FC, FC // 4, 4).swapaxes(2, 3).reshape(x.shape[0], FF)


def up_columns_back(x):
    return x.reshape(x.shape[0], FF // FC, 4, FC // 4).swapaxes(2, 3).reshape(x.shape[0], FF)


def per_device(
    block_input, doc_lengths, cotangent,
    weight_query, weight_keyval, weight_output, weight_expand, weight_reduce,
    momentum_query, momentum_keyval, momentum_output, momentum_expand, momentum_reduce,
    norm_gains, norm_biases, proj_biases, adam_first, adam_second,
):
    grid = Grid()
    chips, narrow = lax.axis_size("chip"), lax.axis_size("narrow")
    devices = 2 * chips * narrow
    core = lax.axis_index("core")
    place = lax.axis_index("chip") * narrow + lax.axis_index("narrow")
    masters = (weight_query, weight_keyval, weight_output, weight_expand, weight_reduce)
    own = D // devices
    up_first = grid.narrow[::-1] + grid.chip[::-1] + [grid.core]
    down_first = grid.narrow[::-1] + grid.chip + [grid.core]

    w_qkv = grid.gather(jnp.concatenate([weight_query, weight_keyval], axis=1).astype(BF), up_first)
    w_out = grid.gather(weight_output.astype(BF), down_first)
    ffn_pack = jnp.concatenate(
        [up_columns(weight_expand), weight_reduce.reshape(own, 4 * D)], axis=1
    ).astype(BF)
    ffn_weights = lax.all_gather(ffn_pack, ("chip", "core", "narrow"), axis=0, tiled=True)
    bias_qkv = proj_biases[:QKV]
    bias_output = proj_biases[QKV : QKV + D]
    bias_expand = proj_biases[QKV + D : QKV + D + FF]
    bias_reduce = proj_biases[QKV + D + FF :]

    n_attn_t, n_ffn, n_ffn_t, g_t = prepare(block_input, cotangent, norm_gains, norm_biases)

    starts, positions = locate(doc_lengths[0])
    frequency = ROPE_BASE ** (-(2.0 * jnp.arange(ROT // 2, dtype=F32)) / ROT)
    angles = positions.astype(F32)[None, :] * frequency[:, None]
    cos, sin = jnp.cos(angles), jnp.sin(angles)
    first_block = starts[::QB] // QB

    qkv_t = dot_tn(w_qkv, n_attn_t) + bias_qkv[:, None]
    grad_mixed_t = dot_nt(w_out, cotangent).astype(BF)
    so_far = attention(first_block, qkv_t, grad_mixed_t, cos, sin, cos, 0, 1, None)
    y, d_ffn, d_up, d_down, d_bias_up = ffn(
        n_ffn, n_ffn_t, cotangent, g_t, ffn_weights, up_columns(bias_expand[None, :]), so_far[0]
    )
    halves = [d.reshape(chips, 2, narrow * own, FF) for d in (d_up, d_down)]
    away = [lax.dynamic_index_in_dim(h, 1 - core, 1, keepdims=False) for h in halves]
    keep = [lax.dynamic_index_in_dim(h, core, 1, keepdims=False) for h in halves]
    halves = [
        (k.astype(F32) + swap(a, "core", 1).astype(F32)).astype(BF) for k, a in zip(keep, away)
    ]
    packed = jnp.concatenate(halves, axis=2).reshape(-1, 2 * FF)
    ffn_grads = lax.psum_scatter(packed, "chip", scatter_dimension=0, tiled=True)

    mix_t, gq_t, _, gkv_t = attention(
        first_block, qkv_t, grad_mixed_t, cos, sin, packed, 1, HEADS // NH - 1, so_far
    )
    ffn_grads, _ = lax.optimization_barrier((ffn_grads, gkv_t))
    ffn_grads = lax.psum_scatter(ffn_grads, "narrow", scatter_dimension=0, tiled=True)
    d_qkv, d_out, bias_sums = grads(cotangent, mix_t, gq_t, gkv_t, n_attn_t)
    scatter_up = [grid.core] + grid.chip + grid.narrow
    scatter_down = [grid.core] + grid.chip[::-1] + grid.narrow
    qkv_sum, passed = grid.scatter(d_qkv, scatter_up)
    out_sum, _ = grid.scatter(d_out, scatter_down)
    ffn_grads = lax.optimization_barrier((ffn_grads, passed[len(grid.chip)]))[0].astype(F32)
    block_output, input_grad, sums = final(
        block_input, cotangent, y, d_ffn, mix_t, gq_t, gkv_t, w_qkv.T, w_out,
        norm_gains, (bias_output + bias_reduce)[None, :],
    )
    vector_grad = jnp.concatenate(
        [sums[0], sums[1], sums[2], sums[3], bias_sums[0], sums[4], up_columns_back(d_bias_up)[0], sums[4]]
    )
    for step in up_first:
        vector_grad = vector_grad + grid.swap(vector_grad, step)

    new_expand = MUON_MOMENTUM * momentum_expand + up_columns_back(ffn_grads[:, :FF])
    new_reduce = MUON_MOMENTUM * momentum_reduce + ffn_grads[:, FF:].reshape(-1, D)
    new_query = MUON_MOMENTUM * momentum_query + qkv_sum[:, :D]
    new_keyval = MUON_MOMENTUM * momentum_keyval + qkv_sum[:, D:QKV]
    new_output = MUON_MOMENTUM * momentum_output + out_sum

    def for_core(first, second):
        mine = jnp.where(core == 0, first, second)
        theirs = swap(jnp.where(core == 0, second, first), "core", 1)
        return jnp.concatenate(
            [jnp.where(core == 0, mine, theirs), jnp.where(core == 0, theirs, mine)], axis=0
        )

    rank = (lax.axis_index("chip") * 2 + core) * narrow + lax.axis_index("narrow")
    sibling = rank + (1 - 2 * core) * narrow

    def both_rows(m):
        return jnp.concatenate(
            [lax.dynamic_slice_in_dim(m, r * own, own, 0) for r in (rank, sibling)], axis=0
        )

    ffn_whole = lax.all_gather(
        jnp.concatenate([new_expand, new_reduce.reshape(own, 4 * D)], axis=1).astype(BF),
        ("chip", "core", "narrow"), axis=0, tiled=True,
    )
    u, q0 = wide_ns(core.astype(jnp.int32).reshape(1), ffn_whole)
    rows_m = both_rows(ffn_whole)
    as_up = dot(both_rows(u), ffn_whole[:, :FF])
    as_down = jnp.concatenate(
        [dot(rows_m[:, FF + q * D : FF + (q + 1) * D], u) for q in range(4)], axis=1
    )
    rows_m = rows_m.astype(F32) * q0[0, 0]
    rows_o = jnp.where(core == 0, rows_m[:, :FF] + as_up, rows_m[:, FF:] + as_down)
    mine, theirs = rows_o[:own], swap(rows_o[own:], "core", 1)
    o_expand = jnp.where(core == 0, mine, theirs)
    o_reduce = jnp.where(core == 0, theirs, mine).reshape(-1, D)

    low_keyval = new_keyval.astype(BF)
    pair = for_core(
        jnp.concatenate([new_query.astype(BF), low_keyval], axis=1),
        jnp.concatenate([new_output.astype(BF), low_keyval], axis=1),
    )
    wide = 512
    whole = jnp.concatenate(
        [
            grid.gather(pair[:, :wide], grid.narrow[::-1] + grid.chip[::-1]),
            grid.gather(pair[:, wide:], grid.narrow[::-1] + grid.chip),
        ],
        axis=1,
    )
    o_pair, o_kv = square_ns(whole[:, :D], whole[:, D:QKV])
    row_lo = place * (2 * own)
    mine = lax.dynamic_slice_in_dim(o_pair, row_lo + core * own, own, 0)
    theirs = swap(lax.dynamic_slice_in_dim(o_pair, row_lo + (1 - core) * own, own, 0), "core", 1)
    o_query = jnp.where(core == 0, mine, theirs)
    o_output = jnp.where(core == 0, theirs, mine)
    o_keyval = lax.dynamic_slice_in_dim(o_kv, row_lo + core * own, own, 0)

    new_momenta = (new_query, new_keyval, new_output, new_expand, new_reduce)
    new_weights = []
    for master, o in zip(masters, (o_query, o_keyval, o_output, o_expand, o_reduce)):
        factor = math.sqrt(max(1.0, master.shape[0] * devices / master.shape[1]))
        new_weights.append(master - MUON_RATE * factor * o)

    params = jnp.concatenate([norm_gains.reshape(-1), norm_biases.reshape(-1), proj_biases])
    vector_first = BETA_FIRST * adam_first + (1.0 - BETA_FIRST) * vector_grad
    vector_second = BETA_SECOND * adam_second + (1.0 - BETA_SECOND) * vector_grad * vector_grad
    corrected_first = vector_first / (1.0 - BETA_FIRST**STEP)
    corrected_second = vector_second / (1.0 - BETA_SECOND**STEP)
    vector_new = params - ADAM_RATE * corrected_first / (jnp.sqrt(corrected_second) + ADAM_EPS)
    return (
        block_output, input_grad, *new_momenta, *new_weights, vector_first, vector_second, vector_new
    )


def solution(mesh):
    wide, narrow = mesh.shape["wide"], mesh.shape["narrow"]
    grid = Mesh(mesh.devices.reshape(wide // 2, 2, narrow), ("chip", "core", "narrow"))
    rows = P(("chip", "core", "narrow"), None)
    in_specs = (rows,) * 13 + (P(),) * 5
    out_specs = (rows,) * 12 + (P(),) * 3
    return jax.shard_map(
        per_device, mesh=grid, in_specs=in_specs, out_specs=out_specs, check_vma=False
    )
```

```python
from functools import partial
import math

import jax
import jax.numpy as jnp
from jax import lax
from jax.experimental import pallas as pl
from jax.experimental.pallas import tpu as pltpu
from jax.sharding import Mesh, PartitionSpec as P

D = 768
HEADS = 12
HEAD_DIM = 64
ROT = 16
FF = 3072
TOK = 2048
NS_STEPS = 5
STEP = 10
QB = 512
HALF = 256
NH = 4
GROUP = NH * HEAD_DIM
FC = 768
BF = jnp.bfloat16
F32 = jnp.float32
LOG2E = 1.4426950408889634
MIB = 1024 * 1024


def dot(a, b):
    return jnp.dot(a, b, preferred_element_type=F32)


def dot_nt(a, b):
    return lax.dot_general(a, b, (((1,), (1,)), ((), ())), preferred_element_type=F32)


def dot_tn(a, b):
    return lax.dot_general(a, b, (((0,), (0,)), ((), ())), preferred_element_type=F32)


def attention_kernel(opening, closing, *refs):
    first_ref, q_ref, do_ref, cos_ref, sin_ref, kv_ref = refs[:6]
    start_ref = None if opening else refs[9]
    refs = refs[7:] if opening else refs[10:]
    mix_ref, dq_ref, dkv_ref = refs[:3]
    refs = refs[3:]
    if closing:
        gkv_ref = refs[0]
        refs = refs[1:]
    (k_ref, kt_ref, vx_ref, vt_ref, qz_ref, e_even, e_odd, acc_ref, m_ref, mh_ref, rhs_ref, dl_ref,
     dqa_ref) = refs
    e_ref = (e_even, e_odd)
    hg = pl.program_id(0)
    qi = pl.program_id(1)
    first = first_ref[qi]
    diag = pl.multiple_of(qi * QB, QB)
    here = pl.ds(diag, QB)

    @pl.when((hg == 0) & (qi == 0))
    def _():
        dkv_ref[...] = jnp.zeros_like(dkv_ref) if opening else start_ref[...]
        filler = jnp.where(lax.broadcasted_iota(jnp.int32, (HEAD_DIM, QB), 0) < 2, 1.0, 0.0)
        for j in range(TOK // QB):
            cols = slice(j * QB, (j + 1) * QB)
            c, s = cos_ref[:, cols], sin_ref[:, cols]
            u = kv_ref[0:HEAD_DIM, cols]
            v = kv_ref[HEAD_DIM:, cols]
            k = jnp.concatenate(
                [u[0:8] * c - u[8:16] * s, u[8:16] * c + u[0:8] * s, u[16:]], axis=0
            )
            kt_ref[:, cols] = k.astype(BF)
            vt_ref[0:HEAD_DIM, cols] = v.astype(BF)
            vt_ref[HEAD_DIM:, cols] = jnp.ones((16, QB), BF)
            both = jnp.concatenate([k, v], axis=0).T
            k_ref[cols, :] = both[:, 0:HEAD_DIM].astype(BF)
            vx_ref[cols, :] = jnp.concatenate([filler, v], axis=0).T.astype(BF)

    cos = cos_ref[:, here]
    sin = sin_ref[:, here]
    scale = LOG2E / math.sqrt(HEAD_DIM)
    for h in range(NH):
        u = q_ref[h * HEAD_DIM : (h + 1) * HEAD_DIM, :]
        a, b = u[0:8], u[8:16]
        turned = jnp.concatenate([a * cos - b * sin, b * cos + a * sin, u[16:]], axis=0)
        qz_ref[h, 0:HEAD_DIM, :] = (turned * scale).astype(BF)
        qz_ref[h, HEAD_DIM:, :] = jnp.zeros((HEAD_DIM, QB), BF)

    def edge_mask(c):
        shape = ((c + 1) * HALF, HALF)
        keys_in = lax.broadcasted_iota(jnp.int32, shape, 0)
        return keys_in <= lax.broadcasted_iota(jnp.int32, shape, 1) + c * HALF

    row16 = lax.broadcasted_iota(jnp.int32, (HEAD_DIM, QB), 0)
    zeros = jnp.zeros((HEAD_DIM, QB), BF)

    def edges(h, c):
        q = qz_ref[h, 0:HEAD_DIM, c * HALF : (c + 1) * HALF]
        s = dot(k_ref[pl.ds(diag, (c + 1) * HALF), :], q)
        return jnp.where(edge_mask(c), s, -1e30)

    def forward_diagonal(h, s, c):
        cols = slice(c * HALF, (c + 1) * HALF)
        rows = pl.ds(diag, (c + 1) * HALF)
        m = jnp.max(s, axis=0, keepdims=True)
        e = jnp.exp2(s - m).astype(BF)
        e_ref[h % 2][rows, cols] = e
        acc_ref[h, :, cols] = dot(vt_ref[:, rows], e)
        m_ref[h, :, cols] = m

    def forward(h, s, off, j):
        m_old = m_ref[h]
        m = jnp.maximum(m_old, jnp.max(s, axis=0, keepdims=True))
        e = jnp.exp2(s - m).astype(BF)
        e_ref[h % 2][pl.ds(off, QB), :] = e
        acc_ref[h] = acc_ref[h] * jnp.exp2(m_old - m) + dot(vt_ref[:, pl.ds(off, QB)], e)
        m_ref[h] = m
        mh_ref[j, h] = m

    def between(h):
        rows = slice(h * HEAD_DIM, (h + 1) * HEAD_DIM)
        inv = 1.0 / acc_ref[h, HEAD_DIM : HEAD_DIM + 1, :]
        mixed = acc_ref[h, 0:HEAD_DIM, :] * inv
        mix_ref[rows, :] = mixed.astype(BF)
        do = do_ref[rows, :].astype(F32)
        delta = jnp.sum(do * mixed, axis=0, keepdims=True)
        rhs_ref[h] = do * inv
        dl_ref[h] = -(delta * inv)

    def scaled(h, j):
        r = jnp.exp2(mh_ref[j, h] - m_ref[h])
        dop = (rhs_ref[h] * r).astype(BF)
        dl = dl_ref[h] * r
        hi = dl.astype(BF).astype(F32)
        lo = dl - hi
        head = jnp.where(row16 == 0, hi, jnp.where(row16 == 1, lo, 0.0)).astype(BF)
        return jnp.concatenate([head, dop], axis=0), jnp.concatenate([zeros, dop], axis=0)

    def backward_diagonal(h, rhs, rz, c):
        cols = slice(c * HALF, (c + 1) * HALF)
        rows = pl.ds(diag, (c + 1) * HALF)
        x = dot(vx_ref[rows, :], rhs[:, cols])
        e = e_ref[h % 2][rows, cols]
        ds = e * x.astype(BF)
        dqa_ref[h, :, cols] = dot(kt_ref[:, rows], ds)
        dkv_ref[rows, :] += dot_nt(ds, qz_ref[h, :, cols]) + dot_nt(e, rz[:, cols])

    def backward(h, x, rz, off):
        e = e_ref[h % 2][pl.ds(off, QB), :]
        ds = e * x.astype(BF)
        dqa_ref[h] += dot(kt_ref[:, pl.ds(off, QB)], ds)
        dkv_ref[pl.ds(off, QB), :] += dot_nt(ds, qz_ref[h]) + dot_nt(e, rz)

    for h in range(NH + 1):
        ahead, behind = h < NH, h > 0
        if behind:
            rhs, rz = scaled(h - 1, qi)
        for c in range(2):
            if ahead:
                parts = edges(h, c)
            if behind:
                backward_diagonal(h - 1, rhs, rz, c)
            if ahead:
                forward_diagonal(h, parts, c)
        if ahead:
            mh_ref[qi, h] = m_ref[h]

        def block(j, carry, h=h, ahead=ahead, behind=behind):
            off = pl.multiple_of(j * QB, QB)
            if ahead:
                s = dot(k_ref[pl.ds(off, QB), :], qz_ref[h, 0:HEAD_DIM, :])
            if behind:
                rhs, rz = scaled(h - 1, j)
                x = dot(vx_ref[pl.ds(off, QB), :], rhs)
                backward(h - 1, x, rz, off)
            if ahead:
                forward(h, s, off, j)
            return carry

        lax.fori_loop(first, qi, block, 0)
        if ahead:
            between(h)

    for h in range(NH):
        u = dqa_ref[h] * (1.0 / math.sqrt(HEAD_DIM))
        a, b = u[0:8], u[8:16]
        turned = jnp.concatenate([a * cos + b * sin, b * cos - a * sin, u[16:]], axis=0)
        dq_ref[h * HEAD_DIM : (h + 1) * HEAD_DIM, :] = turned.astype(BF)

    if closing:

        @pl.when((hg == pl.num_programs(0) - 1) & (qi == pl.num_programs(1) - 1))
        def _():
            for j in range(TOK // QB):
                cols = slice(j * QB, (j + 1) * QB)
                c, s = cos_ref[:, cols], sin_ref[:, cols]
                t = dkv_ref[cols, :].T
                u = t[0:HEAD_DIM] * math.log(2.0)
                k = jnp.concatenate(
                    [u[0:8] * c + u[8:16] * s, u[8:16] * c - u[0:8] * s, u[16:], t[HEAD_DIM:]], axis=0
                )
                gkv_ref[:, cols] = k.astype(BF)


def attention(first, qkv_t, grad_mixed, cos, sin, after, group_lo, groups, so_far):
    blocks = TOK // QB
    opening, closing = so_far is None, (group_lo + groups) * GROUP == D
    group_block = pl.BlockSpec((GROUP, QB), lambda g, i, f: (group_lo + g, i))

    def whole(shape, row=0):
        return pl.BlockSpec(shape, lambda g, i, f: (row, 0))

    anywhere = pl.BlockSpec(memory_space=pl.ANY)
    in_specs = [
        group_block, group_block, whole((8, TOK)), whole((8, TOK)), whole((128, TOK), D // 128), anywhere,
    ]
    operands = [first, qkv_t, grad_mixed, cos, sin, qkv_t, after]
    aliases = {}
    if not opening:
        in_specs += [anywhere, anywhere, whole((TOK, 128))]
        operands += list(so_far)
        aliases = {7: 0, 8: 1}
    out_specs = [group_block, group_block, whole((TOK, 128))]
    out_shape = [
        jax.ShapeDtypeStruct((D, TOK), BF),
        jax.ShapeDtypeStruct((D, TOK), BF),
        jax.ShapeDtypeStruct((TOK, 128), F32),
    ]
    if closing:
        out_specs.append(whole((128, TOK)))
        out_shape.append(jax.ShapeDtypeStruct((128, TOK), BF))
    return pl.pallas_call(
        partial(attention_kernel, opening, closing),
        grid_spec=pltpu.PrefetchScalarGridSpec(
            num_scalar_prefetch=1,
            grid=(groups, blocks),
            in_specs=in_specs,
            out_specs=out_specs,
            scratch_shapes=[
                pltpu.VMEM((TOK, HEAD_DIM), BF),
                pltpu.VMEM((HEAD_DIM, TOK), BF),
                pltpu.VMEM((TOK, 128), BF),
                pltpu.VMEM((80, TOK), BF),
                pltpu.VMEM((NH, 128, QB), BF),
                pltpu.VMEM((TOK, QB), BF),
                pltpu.VMEM((TOK, QB), BF),
                pltpu.VMEM((NH, 80, QB), F32),
                pltpu.VMEM((NH, 1, QB), F32),
                pltpu.VMEM((blocks, NH, 1, QB), F32),
                pltpu.VMEM((NH, HEAD_DIM, QB), F32),
                pltpu.VMEM((NH, 1, QB), F32),
                pltpu.VMEM((NH, HEAD_DIM, QB), F32),
            ],
        ),
        out_shape=out_shape,
        input_output_aliases=aliases,
        compiler_params=pltpu.CompilerParams(
            dimension_semantics=("arbitrary", "arbitrary"), vmem_limit_bytes=48 * MIB
        ),
        cost_estimate=pl.CostEstimate(
            flops=groups * NH * 6 * 2 * TOK * TOK // 2 * 256,
            bytes_accessed=groups * GROUP * TOK * 10,
            transcendentals=groups * NH * TOK * TOK // 2,
        ),
        name="attention",
    )(*operands)


ERF = (0.254829592, -0.284496736, 1.421413741, -1.453152027, 1.061405429)


def gelu_pair(x):
    e = jnp.exp2(x * x * (-0.5 * LOG2E))
    den = 1.0 + (0.3275911 / math.sqrt(2.0)) * jnp.abs(x)
    t = 1.0 / den
    p = ERF[4]
    for c in (ERF[3], ERF[2], ERF[1], ERF[0]):
        p = p * t + c
    tail = (0.5 * p) * (t * e)
    phi = jnp.where(x >= 0.0, 1.0 - tail, tail)
    return phi, phi + x * (e * (1.0 / math.sqrt(2.0 * math.pi)))


def ffn_kernel(
    x_ref, xt_ref, g_ref, gt_ref, up_ref, down_ref, bias_ref, _,
    y_ref, dx_ref, dup_ref, ddown_ref, db_ref,
    pre_ref, grad_ref, act_ref, de_ref, dn_ref,
):
    tile = TOK // 2
    part = 256

    @pl.when(pl.program_id(0) == 0)
    def _():
        y_ref[...] = jnp.zeros_like(y_ref)
        dx_ref[...] = jnp.zeros_like(dx_ref)

    fold = FC // 4
    for q in range(4):
        dn_ref[q * fold : (q + 1) * fold, :] = down_ref[:, q * D : (q + 1) * D]

    for t in range(TOK // tile):
        rows = slice(t * tile, (t + 1) * tile)
        pre_ref[rows, :] = dot(x_ref[rows, :], up_ref[...])
        grad_ref[rows, :] = dot_nt(g_ref[rows, :], dn_ref[...])
    db = jnp.zeros((1, FC), F32)
    for t in range(TOK // tile):
        rows = slice(t * tile, (t + 1) * tile)
        for lo in range(t * tile, (t + 1) * tile, part):
            some = slice(lo, lo + part)
            pre = pre_ref[some, :] + bias_ref[...]
            phi, slope = gelu_pair(pre)
            act_ref[some, :] = (pre * phi).astype(BF)
            d = slope * grad_ref[some, :]
            db = db + jnp.sum(d, axis=0, keepdims=True)
            de_ref[some, :] = d.astype(BF)
        y_ref[rows, :] += dot(act_ref[rows, :], dn_ref[...])
        dx_ref[rows, :] += dot_nt(de_ref[rows, :], up_ref[...])
    db_ref[...] = db
    dup_ref[...] = dot(xt_ref[...], de_ref[...]).astype(BF)
    dd = dot(gt_ref[...], act_ref[...]).T.astype(BF)
    for q in range(4):
        ddown_ref[:, q * D : (q + 1) * D] = dd[q * fold : (q + 1) * fold, :]


def ffn(x, xt, g, gt, weights, bias, after):
    once = pl.Buffered(1)

    def whole(shape):
        return pl.BlockSpec(shape, lambda c: (0, 0), pipeline_mode=once)

    return pl.pallas_call(
        ffn_kernel,
        grid=(FF // FC,),
        in_specs=[
            whole((TOK, D)), whole((D, TOK)), whole((TOK, D)), whole((D, TOK)),
            pl.BlockSpec((D, FC), lambda c: (0, c)),
            pl.BlockSpec((FC // 4, FF), lambda c: (c, 1)),
            pl.BlockSpec((1, FC), lambda c: (0, c)),
            pl.BlockSpec(memory_space=pl.ANY),
        ],
        out_specs=[
            whole((TOK, D)), whole((TOK, D)),
            pl.BlockSpec((D, FC), lambda c: (0, c)),
            pl.BlockSpec((FC // 4, FF), lambda c: (c, 0)),
            pl.BlockSpec((1, FC), lambda c: (0, c)),
        ],
        scratch_shapes=[pltpu.VMEM((TOK, FC), F32)] * 2
        + [pltpu.VMEM((TOK, FC), BF)] * 2 + [pltpu.VMEM((FC, D), BF)],
        out_shape=[
            jax.ShapeDtypeStruct((TOK, D), F32),
            jax.ShapeDtypeStruct((TOK, D), F32),
            jax.ShapeDtypeStruct((D, FF), BF),
            jax.ShapeDtypeStruct((D, FF), BF),
            jax.ShapeDtypeStruct((1, FF), F32),
        ],
        compiler_params=pltpu.CompilerParams(
            dimension_semantics=("arbitrary",), vmem_limit_bytes=58 * MIB
        ),
        cost_estimate=pl.CostEstimate(
            flops=12 * TOK * D * FF, bytes_accessed=44 * MIB, transcendentals=2 * TOK * FF
        ),
        name="ffn",
    )(x, xt, g, gt, weights, weights, bias, after)


ROPE_BASE = 10000.0
NORM_EPS = 1e-05
NS_A, NS_B, NS_C = 3.4445, -4.775, 2.0315
MUON_RATE = 0.5
MUON_MOMENTUM = 0.5
ADAM_RATE = 0.3
BETA_FIRST = 0.9
BETA_SECOND = 0.95
ADAM_EPS = 1e-08
QKV = D + 2 * HEAD_DIM


def merge_kernel(_, up_ref, down_ref, up_in_ref, down_in_ref, out_ref):
    out_ref[:, 0:FF] = (up_ref[...].astype(F32) + up_in_ref[...].astype(F32)).astype(BF)
    out_ref[:, FF:] = (down_ref[...].astype(F32) + down_in_ref[...].astype(F32)).astype(BF)


def merge(core, d_up, d_down, up_in, down_in, rows):
    kept = pl.BlockSpec((rows, FF), lambda i, c: (2 * i + c[0], 0))
    came = pl.BlockSpec((rows, FF), lambda i, c: (i, 0))
    count = up_in.shape[0] // rows
    return pl.pallas_call(
        merge_kernel,
        grid_spec=pltpu.PrefetchScalarGridSpec(
            num_scalar_prefetch=1,
            grid=(count,),
            in_specs=[kept, kept, came, came],
            out_specs=pl.BlockSpec((rows, 2 * FF), lambda i, c: (i, 0)),
        ),
        out_shape=jax.ShapeDtypeStruct((count * rows, 2 * FF), BF),
        compiler_params=pltpu.CompilerParams(vmem_limit_bytes=32 * MIB),
        cost_estimate=pl.CostEstimate(flops=2 * D * FF, bytes_accessed=14 * MIB, transcendentals=0),
        name="merge",
    )(core, d_up, d_down, up_in, down_in)


def prepare_kernel(x_ref, g_ref, gain_ref, shift_ref, na_t_ref, nf_ref, nf_t_ref, g_t_ref):
    x = x_ref[...].astype(F32)
    centred = x - jnp.mean(x, axis=-1, keepdims=True)
    hat = centred * lax.rsqrt(jnp.mean(centred * centred, axis=-1, keepdims=True) + NORM_EPS)
    na_t_ref[...] = (hat * gain_ref[0:1, :] + shift_ref[0:1, :]).T.astype(BF)
    nf = hat * gain_ref[1:2, :] + shift_ref[1:2, :]
    nf_ref[...] = nf.astype(BF)
    nf_t_ref[...] = nf.T.astype(BF)
    g_t_ref[...] = g_ref[...].astype(F32).T.astype(BF)


def prepare(x, g, gains, shifts):
    block = 512
    rows = pl.BlockSpec((block, D), lambda i: (i, 0))
    cols = pl.BlockSpec((D, block), lambda i: (0, i))
    fixed = pl.BlockSpec((2, D), lambda i: (0, 0))
    turned = jax.ShapeDtypeStruct((D, TOK), BF)
    return pl.pallas_call(
        prepare_kernel,
        grid=(TOK // block,),
        in_specs=[rows, rows, fixed, fixed],
        out_specs=[cols, rows, cols, cols],
        out_shape=[turned, jax.ShapeDtypeStruct((TOK, D), BF), turned, turned],
        compiler_params=pltpu.CompilerParams(
            dimension_semantics=("arbitrary",), vmem_limit_bytes=48 * MIB
        ),
        cost_estimate=pl.CostEstimate(
            flops=20 * TOK * D, bytes_accessed=12 * TOK * D, transcendentals=TOK
        ),
        name="prepare",
    )(x, g, gains, shifts)


def grads_kernel(g_ref, mix_ref, gq_ref, gkv_ref, nt_ref, _, dqkv_ref, dout_ref, bsum_ref, qkv_acc, out_acc):
    i = pl.program_id(0)
    gq = gq_ref[...]
    gkv = gkv_ref[...]
    nt = nt_ref[...]

    @pl.when(i == 0)
    def _():
        qkv_acc[...] = jnp.zeros_like(qkv_acc)
        out_acc[...] = jnp.zeros_like(out_acc)
        bsum_ref[...] = jnp.zeros_like(bsum_ref)

    qkv_acc[:, 0:D] += dot_nt(nt, gq)
    qkv_acc[:, D:] += dot_nt(nt, gkv)
    out_acc[...] += dot(mix_ref[...], g_ref[...])
    ones = jnp.ones((8, gq.shape[1]), BF)
    bsum_ref[:, 0:D] += dot_nt(ones, gq)
    bsum_ref[:, D:] += dot_nt(ones, gkv)

    @pl.when(i == pl.num_programs(0) - 1)
    def _():
        dqkv_ref[...] = qkv_acc[...].astype(BF)
        dout_ref[...] = out_acc[...].astype(BF)


def grads(g, mix, gq, gkv, nt, after):
    block = 1024
    cols = pl.BlockSpec((D, block), lambda i: (0, i))

    def fixed(shape):
        return pl.BlockSpec(shape, lambda i: (0, 0))

    return pl.pallas_call(
        grads_kernel,
        grid=(TOK // block,),
        in_specs=[
            pl.BlockSpec((block, D), lambda i: (i, 0)), cols, cols,
            pl.BlockSpec((128, block), lambda i: (0, i)), cols, pl.BlockSpec(memory_space=pl.ANY),
        ],
        out_specs=[fixed((D, QKV)), fixed((D, D)), fixed((8, QKV))],
        scratch_shapes=[pltpu.VMEM((D, QKV), F32), pltpu.VMEM((D, D), F32)],
        out_shape=[
            jax.ShapeDtypeStruct((D, QKV), BF), jax.ShapeDtypeStruct((D, D), BF),
            jax.ShapeDtypeStruct((8, QKV), F32),
        ],
        compiler_params=pltpu.CompilerParams(
            dimension_semantics=("arbitrary",), vmem_limit_bytes=48 * MIB
        ),
        cost_estimate=pl.CostEstimate(
            flops=2 * TOK * D * (QKV + D), bytes_accessed=16 * MIB, transcendentals=0
        ),
        name="grads",
    )(g, mix, gq, gkv, nt, after)


def final_kernel(
    x_ref, g_ref, y_ref, df_ref, mix_ref, gq_ref, gkv_ref, wt_ref, wo_ref, gain_ref, bias_ref, _,
    out_ref, ig_ref, sums_ref,
):
    i = pl.program_id(0)
    x = x_ref[...].astype(F32)
    gf = g_ref[...].astype(F32)

    @pl.when(i == 0)
    def _():
        sums_ref[...] = jnp.zeros_like(sums_ref)

    da = dot_tn(gq_ref[...], wt_ref[0:D, :]) + dot_tn(gkv_ref[...], wt_ref[D:, :])
    out_ref[...] = (x + (dot_tn(mix_ref[...], wo_ref[...]) + y_ref[...] + bias_ref[...])).astype(BF)
    mean = jnp.mean(x, axis=-1, keepdims=True)
    centred = x - mean
    rstd = lax.rsqrt(jnp.mean(centred * centred, axis=-1, keepdims=True) + NORM_EPS)
    hat = centred * rstd
    df = df_ref[...]
    d_hat = da * gain_ref[0:1, :] + df * gain_ref[1:2, :]
    m1 = jnp.mean(d_hat, axis=-1, keepdims=True)
    m2 = jnp.mean(d_hat * hat, axis=-1, keepdims=True)
    ig_ref[...] = gf + rstd * (d_hat - m1 - hat * m2)
    for r, v in enumerate((da * hat, df * hat, da, df, gf)):
        sums_ref[r : r + 1, :] += jnp.sum(v, axis=0, keepdims=True)


def final(x, g, y, d_ffn, mix, gq, gkv, wt, wo, gains, bias, after):
    block = 512

    def rows(i):
        return (i, 0)

    def cols(i):
        return (0, i)

    def fixed(i):
        return (0, 0)

    return pl.pallas_call(
        final_kernel,
        grid=(TOK // block,),
        in_specs=[
            pl.BlockSpec((block, D), rows), pl.BlockSpec((block, D), rows),
            pl.BlockSpec((block, D), rows), pl.BlockSpec((block, D), rows),
            pl.BlockSpec((D, block), cols), pl.BlockSpec((D, block), cols),
            pl.BlockSpec((128, block), cols),
            pl.BlockSpec((QKV, D), fixed), pl.BlockSpec((D, D), fixed),
            pl.BlockSpec((2, D), fixed), pl.BlockSpec((1, D), fixed), pl.BlockSpec(memory_space=pl.ANY),
        ],
        out_specs=[
            pl.BlockSpec((block, D), rows), pl.BlockSpec((block, D), rows), pl.BlockSpec((8, D), fixed),
        ],
        out_shape=[
            jax.ShapeDtypeStruct((TOK, D), BF), jax.ShapeDtypeStruct((TOK, D), F32),
            jax.ShapeDtypeStruct((8, D), F32),
        ],
        compiler_params=pltpu.CompilerParams(
            dimension_semantics=("arbitrary",), vmem_limit_bytes=48 * MIB
        ),
        cost_estimate=pl.CostEstimate(
            flops=2 * TOK * D * (QKV + D), bytes_accessed=36 * MIB, transcendentals=TOK
        ),
        name="closing",
    )(x, g, y, d_ffn, mix, gq, gkv, wt, wo, gains, bias, after)


def eye_block(rows, n, row_lo):
    r = lax.broadcasted_iota(jnp.int32, (rows, n), 0) + row_lo
    return r == lax.broadcasted_iota(jnp.int32, (rows, n), 1)


def diagonal_sum(ref, n, blk):
    total = 0.0
    for r in range(0, n, blk):
        total += jnp.sum(jnp.where(eye_block(blk, blk, 0), ref[r : r + blk, r : r + blk], 0.0))
    return total


def shift_diagonal(ref, low_ref, level, n, blk):
    for r in range(0, n, blk):
        ref[r : r + blk, r : r + blk] -= jnp.where(eye_block(blk, blk, 0), level, 0.0)
        low_ref[r : r + blk, :] = ref[r : r + blk, :].astype(BF)


def recentre(ref, low_ref, n, blk):
    level = diagonal_sum(ref, n, blk) / n
    shift_diagonal(ref, low_ref, level, n, blk)
    return level


def gram_sweep(level, q0, n, blk, a, al, s, sl, t, tl, u, ul, first=False, last=False):
    p0 = NS_A + NS_B * level + NS_C * level * level
    s[...] = (NS_B + 2.0 * NS_C * level) * a[...] + NS_C * dot(al[...], al[...])
    sl[...] = s[...].astype(BF)
    if first:
        u[...] = s[...]
        q0 = p0
    else:
        u[...] = p0 * u[...] + q0 * s[...] + dot(sl[...], ul[...])
        q0 = p0 * q0
    q0 = q0 + recentre(u, ul, n, blk)
    if last:
        return level, q0
    t[...] = p0 * a[...] + level * s[...] + dot(sl[...], al[...])
    t0 = p0 * level + recentre(t, tl, n, blk)
    a[...] = p0 * t[...] + t0 * s[...] + dot(sl[...], tl[...])
    return p0 * t0 + recentre(a, al, n, blk), q0


def wide_kernel(down_ref, m_ref, u_ref, q_ref, a, al, s, sl, t, tl, u, ul):
    blk = 256

    @pl.when(down_ref[0] == 0)
    def _():
        a[...] = dot_nt(m_ref[...], m_ref[...])

    @pl.when(down_ref[0] != 0)
    def _():
        for q in range(4):
            part = m_ref[:, q * D : (q + 1) * D]
            if q == 0:
                a[...] = dot_tn(part, part)
            else:
                a[...] += dot_tn(part, part)

    inverse = 1.0 / (jnp.sqrt(jnp.full((1, D), diagonal_sum(a, D, blk))) + 1e-07)
    a[...] = a[...] * (inverse * inverse)
    level = recentre(a, al, D, blk)
    state = (a, al, s, sl, t, tl, u, ul)

    def sweep(k, carry):
        return gram_sweep(carry[0], carry[1], D, blk, *state)

    carry = gram_sweep(level, None, D, blk, *state, first=True)
    carry = lax.fori_loop(1, NS_STEPS - 1, sweep, carry)
    _, q0 = gram_sweep(carry[0], carry[1], D, blk, *state, last=True)
    u_ref[...] = (u[...] * inverse).astype(BF)
    q_ref[...] = q0 * inverse


def wide_ns(down, m):
    big, low = pltpu.VMEM((D, D), F32), pltpu.VMEM((D, D), BF)

    def fixed(i, d):
        return (0, 0)

    return pl.pallas_call(
        wide_kernel,
        grid_spec=pltpu.PrefetchScalarGridSpec(
            num_scalar_prefetch=1,
            grid=(1,),
            in_specs=[pl.BlockSpec((D, FF), lambda i, d: (0, d[0]), pipeline_mode=pl.Buffered(1))],
            out_specs=[pl.BlockSpec((D, D), fixed), pl.BlockSpec((1, D), fixed)],
            scratch_shapes=[big, low] * 4,
        ),
        out_shape=[jax.ShapeDtypeStruct((D, D), BF), jax.ShapeDtypeStruct((1, D), F32)],
        compiler_params=pltpu.CompilerParams(vmem_limit_bytes=48 * MIB),
        cost_estimate=pl.CostEstimate(flops=2 * 24 * D**3, bytes_accessed=6 * MIB, transcendentals=D),
        name="wide_ns",
    )(down, m)


def square_kernel(m_ref, kv_ref, o_ref, okv_ref, x, xl, a, al, sl, *small):
    blk = 256
    n = 2 * HEAD_DIM
    m = m_ref[...].astype(F32)
    x[...] = m / (jnp.sqrt(jnp.full((1, D), jnp.sum(m * m))) + 1e-07)
    sa, sal, ss, ssl, st, stl, su, sul = small
    kv = kv_ref[...]
    sa[...] = dot_tn(kv, kv)
    inverse = 1.0 / (jnp.sqrt(jnp.full((1, n), diagonal_sum(sa, n, n))) + 1e-07)
    sa[...] = sa[...] * (inverse * inverse)
    su[...] = jnp.zeros_like(su)
    sul[...] = jnp.zeros_like(sul)
    level = recentre(sa, sal, n, n)

    def sweep(k, carry):
        xl[...] = x[...].astype(BF)
        a[...] = dot_nt(xl[...], xl[...])
        lev = recentre(a, al, D, blk)
        p0 = NS_A + NS_B * lev + NS_C * lev * lev
        small_next = gram_sweep(carry[0], carry[1], n, n, sa, sal, ss, ssl, st, stl, su, sul)
        sl[...] = ((NS_B + 2.0 * NS_C * lev) * a[...] + NS_C * dot(al[...], al[...])).astype(BF)
        x[...] = p0 * x[...] + dot(sl[...], xl[...])
        return small_next

    _, q0 = lax.fori_loop(0, NS_STEPS, sweep, (level, jnp.float32(1.0)))
    o_ref[...] = x[...]
    okv_ref[...] = (q0 * kv.astype(F32) + dot(kv, sul[...])) * inverse


def square_ns(m, kv):
    big, low = pltpu.VMEM((D, D), F32), pltpu.VMEM((D, D), BF)
    n = 2 * HEAD_DIM
    return pl.pallas_call(
        square_kernel,
        in_specs=[pl.BlockSpec(memory_space=pltpu.VMEM)] * 2,
        out_specs=[pl.BlockSpec(memory_space=pltpu.VMEM)] * 2,
        scratch_shapes=[big, low, big, low, low]
        + [pltpu.VMEM((n, n), F32), pltpu.VMEM((n, n), BF)] * 4,
        out_shape=[jax.ShapeDtypeStruct((D, D), F32), jax.ShapeDtypeStruct((D, n), F32)],
        compiler_params=pltpu.CompilerParams(vmem_limit_bytes=48 * MIB),
        cost_estimate=pl.CostEstimate(flops=2 * 17 * D**3, bytes_accessed=6 * MIB, transcendentals=D),
        name="square_ns",
    )(m, kv)


def swap(x, axis, bit):
    return lax.ppermute(x, axis, [(i, i ^ bit) for i in range(lax.axis_size(axis))])


def bits_of(size):
    return [1 << b for b in range(size.bit_length() - 1)]


class Grid:
    def __init__(self):
        chip, narrow = bits_of(lax.axis_size("chip")), bits_of(lax.axis_size("narrow"))
        self.axes = [("chip", b) for b in reversed(chip)] + [("core", 1)]
        self.axes += [("narrow", b) for b in reversed(narrow)]
        self.chip = list(range(len(chip)))
        self.core = len(chip)
        self.narrow = list(range(len(chip) + 1, len(self.axes)))

    def bit(self, place):
        axis, bit = self.axes[place]
        return (lax.axis_index(axis) // bit) % 2

    def swap(self, x, place):
        return swap(x, *self.axes[place])

    def gather(self, x, order):
        x = x.reshape((1,) * len(self.axes) + x.shape)
        for place in order:
            other = self.swap(x, place)
            up = self.bit(place) == 1
            x = jnp.concatenate([jnp.where(up, other, x), jnp.where(up, x, other)], axis=place)
        return x.reshape((-1,) + x.shape[len(self.axes) + 1 :])

    def scatter(self, x, order):
        x = x.reshape((2,) * len(self.axes) + (-1,) + x.shape[1:])
        for place in order:
            bit = self.bit(place)
            away = lax.dynamic_index_in_dim(x, 1 - bit, place, keepdims=True).astype(BF)
            keep = lax.dynamic_index_in_dim(x, bit, place, keepdims=True).astype(F32)
            x = keep + self.swap(away, place).astype(F32)
        return x.reshape((-1,) + x.shape[len(self.axes) + 1 :])


def locate(lengths):
    ends = jnp.cumsum(lengths)
    token_ids = jnp.arange(TOK, dtype=jnp.int32)
    starts = jnp.max(jnp.where(ends[None, :] <= token_ids[:, None], ends[None, :], 0), axis=1)
    return starts, token_ids - starts


def up_columns(x):
    return x.reshape(x.shape[0], FF // FC, FC // 4, 4).swapaxes(2, 3).reshape(x.shape[0], FF)


def up_columns_back(x):
    return x.reshape(x.shape[0], FF // FC, 4, FC // 4).swapaxes(2, 3).reshape(x.shape[0], FF)


def per_device(
    block_input, doc_lengths, cotangent,
    weight_query, weight_keyval, weight_output, weight_expand, weight_reduce,
    momentum_query, momentum_keyval, momentum_output, momentum_expand, momentum_reduce,
    norm_gains, norm_biases, proj_biases, adam_first, adam_second,
):
    grid = Grid()
    chips, narrow = lax.axis_size("chip"), lax.axis_size("narrow")
    devices = 2 * chips * narrow
    core = lax.axis_index("core")
    place = lax.axis_index("chip") * narrow + lax.axis_index("narrow")
    masters = (weight_query, weight_keyval, weight_output, weight_expand, weight_reduce)
    own = D // devices
    up_first = grid.narrow[::-1] + grid.chip[::-1] + [grid.core]
    down_first = grid.narrow[::-1] + grid.chip + [grid.core]

    w_qkv = grid.gather(jnp.concatenate([weight_query, weight_keyval], axis=1).astype(BF), up_first)
    w_out = grid.gather(weight_output.astype(BF), down_first)
    ffn_pack = jnp.concatenate(
        [up_columns(weight_expand), weight_reduce.reshape(own, 4 * D)], axis=1
    ).astype(BF)
    ffn_weights = lax.all_gather(ffn_pack, ("chip", "core", "narrow"), axis=0, tiled=True)
    bias_qkv = proj_biases[:QKV]
    bias_output = proj_biases[QKV : QKV + D]
    bias_expand = proj_biases[QKV + D : QKV + D + FF]
    bias_reduce = proj_biases[QKV + D + FF :]

    n_attn_t, n_ffn, n_ffn_t, g_t = prepare(block_input, cotangent, norm_gains, norm_biases)

    starts, positions = locate(doc_lengths[0])
    frequency = ROPE_BASE ** (-(2.0 * jnp.arange(ROT // 2, dtype=F32)) / ROT)
    angles = positions.astype(F32)[None, :] * frequency[:, None]
    cos, sin = jnp.cos(angles), jnp.sin(angles)
    first_block = starts[::QB] // QB

    qkv_t = dot_tn(w_qkv, n_attn_t) + bias_qkv[:, None]
    grad_mixed_t = dot_nt(w_out, cotangent).astype(BF)
    so_far = attention(first_block, qkv_t, grad_mixed_t, cos, sin, cos, 0, 1, None)
    y, d_ffn, d_up, d_down, d_bias_up = ffn(
        n_ffn, n_ffn_t, cotangent, g_t, ffn_weights, up_columns(bias_expand[None, :]), so_far[0]
    )
    came = [
        swap(
            lax.dynamic_index_in_dim(d.reshape(chips, 2, narrow * own, FF), 1 - core, 1, keepdims=False),
            "core", 1,
        ).reshape(D // 2, FF)
        for d in (d_up, d_down)
    ]
    core_id = core.astype(jnp.int32).reshape(1)
    packed = merge(core_id, d_up, d_down, *came, narrow * own)
    ffn_grads = lax.psum_scatter(packed, "chip", scatter_dimension=0, tiled=True)
    so_far = attention(first_block, qkv_t, grad_mixed_t, cos, sin, packed, 1, 1, so_far)
    ffn_grads, _ = lax.optimization_barrier((ffn_grads, so_far[2]))
    mix_t, gq_t, _, gkv_t = attention(
        first_block, qkv_t, grad_mixed_t, cos, sin, ffn_grads, 2, HEADS // NH - 2, so_far
    )
    ffn_grads = lax.psum_scatter(ffn_grads, "narrow", scatter_dimension=0, tiled=True)
    ffn_grads = lax.optimization_barrier((ffn_grads, gkv_t))[0].astype(F32)
    new_expand = MUON_MOMENTUM * momentum_expand + up_columns_back(ffn_grads[:, :FF])
    new_reduce = MUON_MOMENTUM * momentum_reduce + ffn_grads[:, FF:].reshape(-1, D)
    ffn_momenta = jnp.concatenate([new_expand, new_reduce.reshape(own, 4 * D)], axis=1).astype(BF)
    ffn_whole = lax.all_gather(ffn_momenta, ("chip", "core", "narrow"), axis=0, tiled=True)
    d_qkv, d_out, bias_sums = grads(cotangent, mix_t, gq_t, gkv_t, n_attn_t, ffn_momenta)
    scatter_up = [grid.core] + grid.chip + grid.narrow
    scatter_down = [grid.core] + grid.chip[::-1] + grid.narrow
    qkv_sum = grid.scatter(d_qkv, scatter_up)
    out_sum = grid.scatter(d_out, scatter_down)
    block_output, input_grad, sums = final(
        block_input, cotangent, y, d_ffn, mix_t, gq_t, gkv_t, w_qkv.T, w_out,
        norm_gains, (bias_output + bias_reduce)[None, :], bias_sums,
    )
    vector_grad = jnp.concatenate(
        [sums[0], sums[1], sums[2], sums[3], bias_sums[0], sums[4], up_columns_back(d_bias_up)[0], sums[4]]
    )
    for step in up_first:
        vector_grad = vector_grad + grid.swap(vector_grad, step)

    new_query = MUON_MOMENTUM * momentum_query + qkv_sum[:, :D]
    new_keyval = MUON_MOMENTUM * momentum_keyval + qkv_sum[:, D:QKV]
    new_output = MUON_MOMENTUM * momentum_output + out_sum

    def for_core(first, second):
        mine = jnp.where(core == 0, first, second)
        theirs = swap(jnp.where(core == 0, second, first), "core", 1)
        return jnp.concatenate(
            [jnp.where(core == 0, mine, theirs), jnp.where(core == 0, theirs, mine)], axis=0
        )

    rank = (lax.axis_index("chip") * 2 + core) * narrow + lax.axis_index("narrow")
    sibling = rank + (1 - 2 * core) * narrow

    def both_rows(m):
        return jnp.concatenate(
            [lax.dynamic_slice_in_dim(m, r * own, own, 0) for r in (rank, sibling)], axis=0
        )

    u, q0 = wide_ns(core_id, ffn_whole)
    rows_m = both_rows(ffn_whole)
    as_up = dot(both_rows(u), ffn_whole[:, :FF])
    as_down = jnp.concatenate(
        [dot(rows_m[:, FF + q * D : FF + (q + 1) * D], u) for q in range(4)], axis=1
    )
    rows_m = rows_m.astype(F32) * q0[0, 0]
    rows_o = jnp.where(core == 0, rows_m[:, :FF] + as_up, rows_m[:, FF:] + as_down)
    mine, theirs = rows_o[:own], swap(rows_o[own:], "core", 1)
    o_expand = jnp.where(core == 0, mine, theirs)
    o_reduce = jnp.where(core == 0, theirs, mine).reshape(-1, D)

    low_keyval = new_keyval.astype(BF)
    pair = for_core(
        jnp.concatenate([new_query.astype(BF), low_keyval], axis=1),
        jnp.concatenate([new_output.astype(BF), low_keyval], axis=1),
    )
    wide = 512
    whole = jnp.concatenate(
        [
            grid.gather(pair[:, :wide], grid.narrow[::-1] + grid.chip[::-1]),
            grid.gather(pair[:, wide:], grid.narrow[::-1] + grid.chip),
        ],
        axis=1,
    )
    o_pair, o_kv = square_ns(whole[:, :D], whole[:, D:QKV])
    row_lo = place * (2 * own)
    mine = lax.dynamic_slice_in_dim(o_pair, row_lo + core * own, own, 0)
    theirs = swap(lax.dynamic_slice_in_dim(o_pair, row_lo + (1 - core) * own, own, 0), "core", 1)
    o_query = jnp.where(core == 0, mine, theirs)
    o_output = jnp.where(core == 0, theirs, mine)
    o_keyval = lax.dynamic_slice_in_dim(o_kv, row_lo + core * own, own, 0)

    new_momenta = (new_query, new_keyval, new_output, new_expand, new_reduce)
    new_weights = []
    for master, o in zip(masters, (o_query, o_keyval, o_output, o_expand, o_reduce)):
        factor = math.sqrt(max(1.0, master.shape[0] * devices / master.shape[1]))
        new_weights.append(master - MUON_RATE * factor * o)

    params = jnp.concatenate([norm_gains.reshape(-1), norm_biases.reshape(-1), proj_biases])
    vector_first = BETA_FIRST * adam_first + (1.0 - BETA_FIRST) * vector_grad
    vector_second = BETA_SECOND * adam_second + (1.0 - BETA_SECOND) * vector_grad * vector_grad
    corrected_first = vector_first / (1.0 - BETA_FIRST**STEP)
    corrected_second = vector_second / (1.0 - BETA_SECOND**STEP)
    vector_new = params - ADAM_RATE * corrected_first / (jnp.sqrt(corrected_second) + ADAM_EPS)
    return (
        block_output, input_grad, *new_momenta, *new_weights, vector_first, vector_second, vector_new
    )


def solution(mesh):
    wide, narrow = mesh.shape["wide"], mesh.shape["narrow"]
    grid = Mesh(mesh.devices.reshape(wide // 2, 2, narrow), ("chip", "core", "narrow"))
    rows = P(("chip", "core", "narrow"), None)
    in_specs = (rows,) * 13 + (P(),) * 5
    out_specs = (rows,) * 12 + (P(),) * 3
    return jax.shard_map(
        per_device, mesh=grid, in_specs=in_specs, out_specs=out_specs, check_vma=False
    )
```

```python
from functools import partial
import math

import jax
import jax.numpy as jnp
from jax import lax
from jax.experimental import pallas as pl
from jax.experimental.pallas import tpu as pltpu
from jax.sharding import Mesh, PartitionSpec as P

D = 768
HEADS = 12
HEAD_DIM = 64
ROT = 16
FF = 3072
TOK = 2048
NS_STEPS = 5
STEP = 10
QB = 512
HALF = 256
NH = 4
GROUP = NH * HEAD_DIM
FC = 768
BF = jnp.bfloat16
F32 = jnp.float32
LOG2E = 1.4426950408889634
MIB = 1024 * 1024


def dot(a, b):
    return jnp.dot(a, b, preferred_element_type=F32)


def dot_nt(a, b):
    return lax.dot_general(a, b, (((1,), (1,)), ((), ())), preferred_element_type=F32)


def dot_tn(a, b):
    return lax.dot_general(a, b, (((0,), (0,)), ((), ())), preferred_element_type=F32)


def attention_kernel(opening, closing, *refs):
    first_ref, q_ref, do_ref, cos_ref, sin_ref, kv_ref = refs[:6]
    start_ref = None if opening else refs[9]
    refs = refs[7:] if opening else refs[10:]
    mix_ref, dq_ref, dkv_ref = refs[:3]
    refs = refs[3:]
    if closing:
        gkv_ref = refs[0]
        refs = refs[1:]
    (k_ref, kt_ref, vx_ref, vt_ref, qz_ref, e_even, e_odd, acc_ref, m_ref, mh_ref, rhs_ref, dl_ref,
     dqa_ref) = refs
    e_ref = (e_even, e_odd)
    hg = pl.program_id(0)
    qi = pl.program_id(1)
    first = first_ref[qi]
    diag = pl.multiple_of(qi * QB, QB)
    here = pl.ds(diag, QB)

    @pl.when((hg == 0) & (qi == 0))
    def _():
        dkv_ref[...] = jnp.zeros_like(dkv_ref) if opening else start_ref[...]
        filler = jnp.where(lax.broadcasted_iota(jnp.int32, (HEAD_DIM, QB), 0) < 2, 1.0, 0.0)
        for j in range(TOK // QB):
            cols = slice(j * QB, (j + 1) * QB)
            c, s = cos_ref[:, cols], sin_ref[:, cols]
            u = kv_ref[0:HEAD_DIM, cols]
            v = kv_ref[HEAD_DIM:, cols]
            k = jnp.concatenate(
                [u[0:8] * c - u[8:16] * s, u[8:16] * c + u[0:8] * s, u[16:]], axis=0
            )
            kt_ref[:, cols] = k.astype(BF)
            vt_ref[0:HEAD_DIM, cols] = v.astype(BF)
            vt_ref[HEAD_DIM:, cols] = jnp.ones((16, QB), BF)
            both = jnp.concatenate([k, v], axis=0).T
            k_ref[cols, :] = both[:, 0:HEAD_DIM].astype(BF)
            vx_ref[cols, :] = jnp.concatenate([filler, v], axis=0).T.astype(BF)

    cos = cos_ref[:, here]
    sin = sin_ref[:, here]
    scale = LOG2E / math.sqrt(HEAD_DIM)
    for h in range(NH):
        u = q_ref[h * HEAD_DIM : (h + 1) * HEAD_DIM, :]
        a, b = u[0:8], u[8:16]
        turned = jnp.concatenate([a * cos - b * sin, b * cos + a * sin, u[16:]], axis=0)
        qz_ref[h, 0:HEAD_DIM, :] = (turned * scale).astype(BF)
        qz_ref[h, HEAD_DIM:, :] = jnp.zeros((HEAD_DIM, QB), BF)

    def edge_mask(c):
        shape = ((c + 1) * HALF, HALF)
        keys_in = lax.broadcasted_iota(jnp.int32, shape, 0)
        return keys_in <= lax.broadcasted_iota(jnp.int32, shape, 1) + c * HALF

    row16 = lax.broadcasted_iota(jnp.int32, (HEAD_DIM, QB), 0)
    zeros = jnp.zeros((HEAD_DIM, QB), BF)

    def edges(h, c):
        q = qz_ref[h, 0:HEAD_DIM, c * HALF : (c + 1) * HALF]
        s = dot(k_ref[pl.ds(diag, (c + 1) * HALF), :], q)
        return jnp.where(edge_mask(c), s, -1e30)

    def forward_diagonal(h, s, c):
        cols = slice(c * HALF, (c + 1) * HALF)
        rows = pl.ds(diag, (c + 1) * HALF)
        m = jnp.max(s, axis=0, keepdims=True)
        e = jnp.exp2(s - m).astype(BF)
        e_ref[h % 2][rows, cols] = e
        acc_ref[h, :, cols] = dot(vt_ref[:, rows], e)
        m_ref[h, :, cols] = m

    def forward(h, s, off, j):
        m_old = m_ref[h]
        m = jnp.maximum(m_old, jnp.max(s, axis=0, keepdims=True))
        e = jnp.exp2(s - m).astype(BF)
        e_ref[h % 2][pl.ds(off, QB), :] = e
        acc_ref[h] = acc_ref[h] * jnp.exp2(m_old - m) + dot(vt_ref[:, pl.ds(off, QB)], e)
        m_ref[h] = m
        mh_ref[j, h] = m

    def between(h):
        rows = slice(h * HEAD_DIM, (h + 1) * HEAD_DIM)
        inv = 1.0 / acc_ref[h, HEAD_DIM : HEAD_DIM + 1, :]
        mixed = acc_ref[h, 0:HEAD_DIM, :] * inv
        mix_ref[rows, :] = mixed.astype(BF)
        do = do_ref[rows, :].astype(F32)
        delta = jnp.sum(do * mixed, axis=0, keepdims=True)
        rhs_ref[h] = do * inv
        dl_ref[h] = -(delta * inv)

    def scaled(h, j):
        r = jnp.exp2(mh_ref[j, h] - m_ref[h])
        dop = (rhs_ref[h] * r).astype(BF)
        dl = dl_ref[h] * r
        hi = dl.astype(BF).astype(F32)
        lo = dl - hi
        head = jnp.where(row16 == 0, hi, jnp.where(row16 == 1, lo, 0.0)).astype(BF)
        return jnp.concatenate([head, dop], axis=0), jnp.concatenate([zeros, dop], axis=0)

    def backward_diagonal(h, rhs, rz, c):
        cols = slice(c * HALF, (c + 1) * HALF)
        rows = pl.ds(diag, (c + 1) * HALF)
        x = dot(vx_ref[rows, :], rhs[:, cols])
        e = e_ref[h % 2][rows, cols]
        ds = e * x.astype(BF)
        dqa_ref[h, :, cols] = dot(kt_ref[:, rows], ds)
        dkv_ref[rows, :] += dot_nt(ds, qz_ref[h, :, cols]) + dot_nt(e, rz[:, cols])

    def backward(h, x, rz, off):
        e = e_ref[h % 2][pl.ds(off, QB), :]
        ds = e * x.astype(BF)
        dqa_ref[h] += dot(kt_ref[:, pl.ds(off, QB)], ds)
        dkv_ref[pl.ds(off, QB), :] += dot_nt(ds, qz_ref[h]) + dot_nt(e, rz)

    for h in range(NH + 1):
        ahead, behind = h < NH, h > 0
        if behind:
            rhs, rz = scaled(h - 1, qi)
        for c in range(2):
            if ahead:
                parts = edges(h, c)
            if behind:
                backward_diagonal(h - 1, rhs, rz, c)
            if ahead:
                forward_diagonal(h, parts, c)
        if ahead:
            mh_ref[qi, h] = m_ref[h]

        def block(j, carry, h=h, ahead=ahead, behind=behind):
            off = pl.multiple_of(j * QB, QB)
            if ahead:
                s = dot(k_ref[pl.ds(off, QB), :], qz_ref[h, 0:HEAD_DIM, :])
            if behind:
                rhs, rz = scaled(h - 1, j)
                x = dot(vx_ref[pl.ds(off, QB), :], rhs)
                backward(h - 1, x, rz, off)
            if ahead:
                forward(h, s, off, j)
            return carry

        lax.fori_loop(first, qi, block, 0)
        if ahead:
            between(h)

    for h in range(NH):
        u = dqa_ref[h] * (1.0 / math.sqrt(HEAD_DIM))
        a, b = u[0:8], u[8:16]
        turned = jnp.concatenate([a * cos + b * sin, b * cos - a * sin, u[16:]], axis=0)
        dq_ref[h * HEAD_DIM : (h + 1) * HEAD_DIM, :] = turned.astype(BF)

    if closing:

        @pl.when((hg == pl.num_programs(0) - 1) & (qi == pl.num_programs(1) - 1))
        def _():
            for j in range(TOK // QB):
                cols = slice(j * QB, (j + 1) * QB)
                c, s = cos_ref[:, cols], sin_ref[:, cols]
                t = dkv_ref[cols, :].T
                u = t[0:HEAD_DIM] * math.log(2.0)
                k = jnp.concatenate(
                    [u[0:8] * c + u[8:16] * s, u[8:16] * c - u[0:8] * s, u[16:], t[HEAD_DIM:]], axis=0
                )
                gkv_ref[:, cols] = k.astype(BF)


def attention(first, qkv_t, grad_mixed, cos, sin, after, group_lo, groups, so_far):
    blocks = TOK // QB
    opening, closing = so_far is None, (group_lo + groups) * GROUP == D
    group_block = pl.BlockSpec((GROUP, QB), lambda g, i, f: (group_lo + g, i))

    def whole(shape, row=0):
        return pl.BlockSpec(shape, lambda g, i, f: (row, 0))

    anywhere = pl.BlockSpec(memory_space=pl.ANY)
    in_specs = [
        group_block, group_block, whole((8, TOK)), whole((8, TOK)), whole((128, TOK), D // 128), anywhere,
    ]
    operands = [first, qkv_t, grad_mixed, cos, sin, qkv_t, after]
    aliases = {}
    if not opening:
        in_specs += [anywhere, anywhere, whole((TOK, 128))]
        operands += list(so_far)
        aliases = {7: 0, 8: 1}
    out_specs = [group_block, group_block, whole((TOK, 128))]
    out_shape = [
        jax.ShapeDtypeStruct((D, TOK), BF),
        jax.ShapeDtypeStruct((D, TOK), BF),
        jax.ShapeDtypeStruct((TOK, 128), F32),
    ]
    if closing:
        out_specs.append(whole((128, TOK)))
        out_shape.append(jax.ShapeDtypeStruct((128, TOK), BF))
    return pl.pallas_call(
        partial(attention_kernel, opening, closing),
        grid_spec=pltpu.PrefetchScalarGridSpec(
            num_scalar_prefetch=1,
            grid=(groups, blocks),
            in_specs=in_specs,
            out_specs=out_specs,
            scratch_shapes=[
                pltpu.VMEM((TOK, HEAD_DIM), BF),
                pltpu.VMEM((HEAD_DIM, TOK), BF),
                pltpu.VMEM((TOK, 128), BF),
                pltpu.VMEM((80, TOK), BF),
                pltpu.VMEM((NH, 128, QB), BF),
                pltpu.VMEM((TOK, QB), BF),
                pltpu.VMEM((TOK, QB), BF),
                pltpu.VMEM((NH, 80, QB), F32),
                pltpu.VMEM((NH, 1, QB), F32),
                pltpu.VMEM((blocks, NH, 1, QB), F32),
                pltpu.VMEM((NH, HEAD_DIM, QB), F32),
                pltpu.VMEM((NH, 1, QB), F32),
                pltpu.VMEM((NH, HEAD_DIM, QB), F32),
            ],
        ),
        out_shape=out_shape,
        input_output_aliases=aliases,
        compiler_params=pltpu.CompilerParams(
            dimension_semantics=("arbitrary", "arbitrary"), vmem_limit_bytes=48 * MIB
        ),
        cost_estimate=pl.CostEstimate(
            flops=groups * NH * 6 * 2 * TOK * TOK // 2 * 256,
            bytes_accessed=groups * GROUP * TOK * 10,
            transcendentals=groups * NH * TOK * TOK // 2,
        ),
        name="attention",
    )(*operands)


ERF = (0.254829592, -0.284496736, 1.421413741, -1.453152027, 1.061405429)


def gelu_pair(x):
    e = jnp.exp2(x * x * (-0.5 * LOG2E))
    den = 1.0 + (0.3275911 / math.sqrt(2.0)) * jnp.abs(x)
    t = 1.0 / den
    p = ERF[4]
    for c in (ERF[3], ERF[2], ERF[1], ERF[0]):
        p = p * t + c
    tail = (0.5 * p) * (t * e)
    phi = jnp.where(x >= 0.0, 1.0 - tail, tail)
    return phi, phi + x * (e * (1.0 / math.sqrt(2.0 * math.pi)))


def ffn_kernel(
    x_ref, xt_ref, g_ref, gt_ref, up_ref, down_ref, bias_ref, _,
    y_ref, dx_ref, dup_ref, ddown_ref, db_ref,
    pre_ref, grad_ref, act_ref, de_ref, dn_ref,
):
    tile = TOK // 2
    part = 256

    @pl.when(pl.program_id(0) == 0)
    def _():
        y_ref[...] = jnp.zeros_like(y_ref)
        dx_ref[...] = jnp.zeros_like(dx_ref)

    fold = FC // 4
    for q in range(4):
        dn_ref[q * fold : (q + 1) * fold, :] = down_ref[:, q * D : (q + 1) * D]

    for t in range(TOK // tile):
        rows = slice(t * tile, (t + 1) * tile)
        pre_ref[rows, :] = dot(x_ref[rows, :], up_ref[...])
        grad_ref[rows, :] = dot_nt(g_ref[rows, :], dn_ref[...])
    db = jnp.zeros((1, FC), F32)
    for t in range(TOK // tile):
        rows = slice(t * tile, (t + 1) * tile)
        for lo in range(t * tile, (t + 1) * tile, part):
            some = slice(lo, lo + part)
            pre = pre_ref[some, :] + bias_ref[...]
            phi, slope = gelu_pair(pre)
            act_ref[some, :] = (pre * phi).astype(BF)
            d = slope * grad_ref[some, :]
            db = db + jnp.sum(d, axis=0, keepdims=True)
            de_ref[some, :] = d.astype(BF)
        y_ref[rows, :] += dot(act_ref[rows, :], dn_ref[...])
        dx_ref[rows, :] += dot_nt(de_ref[rows, :], up_ref[...])
    db_ref[...] = db
    dup_ref[...] = dot(xt_ref[...], de_ref[...]).astype(BF)
    dd = dot(gt_ref[...], act_ref[...]).T.astype(BF)
    for q in range(4):
        ddown_ref[:, q * D : (q + 1) * D] = dd[q * fold : (q + 1) * fold, :]


def ffn(x, xt, g, gt, weights, bias, after):
    once = pl.Buffered(1)

    def whole(shape):
        return pl.BlockSpec(shape, lambda c: (0, 0), pipeline_mode=once)

    return pl.pallas_call(
        ffn_kernel,
        grid=(FF // FC,),
        in_specs=[
            whole((TOK, D)), whole((D, TOK)), whole((TOK, D)), whole((D, TOK)),
            pl.BlockSpec((D, FC), lambda c: (0, c)),
            pl.BlockSpec((FC // 4, FF), lambda c: (c, 1)),
            pl.BlockSpec((1, FC), lambda c: (0, c)),
            pl.BlockSpec(memory_space=pl.ANY),
        ],
        out_specs=[
            whole((TOK, D)), whole((TOK, D)),
            pl.BlockSpec((D, FC), lambda c: (0, c)),
            pl.BlockSpec((FC // 4, FF), lambda c: (c, 0)),
            pl.BlockSpec((1, FC), lambda c: (0, c)),
        ],
        scratch_shapes=[pltpu.VMEM((TOK, FC), F32)] * 2
        + [pltpu.VMEM((TOK, FC), BF)] * 2 + [pltpu.VMEM((FC, D), BF)],
        out_shape=[
            jax.ShapeDtypeStruct((TOK, D), F32),
            jax.ShapeDtypeStruct((TOK, D), F32),
            jax.ShapeDtypeStruct((D, FF), BF),
            jax.ShapeDtypeStruct((D, FF), BF),
            jax.ShapeDtypeStruct((1, FF), F32),
        ],
        compiler_params=pltpu.CompilerParams(
            dimension_semantics=("arbitrary",), vmem_limit_bytes=58 * MIB
        ),
        cost_estimate=pl.CostEstimate(
            flops=12 * TOK * D * FF, bytes_accessed=44 * MIB, transcendentals=2 * TOK * FF
        ),
        name="ffn",
    )(x, xt, g, gt, weights, weights, bias, after)


ROPE_BASE = 10000.0
NORM_EPS = 1e-05
NS_A, NS_B, NS_C = 3.4445, -4.775, 2.0315
MUON_RATE = 0.5
MUON_MOMENTUM = 0.5
ADAM_RATE = 0.3
BETA_FIRST = 0.9
BETA_SECOND = 0.95
ADAM_EPS = 1e-08
QKV = D + 2 * HEAD_DIM


def merge_kernel(_, up_ref, down_ref, up_in_ref, down_in_ref, out_ref):
    out_ref[:, 0:FF] = (up_ref[...].astype(F32) + up_in_ref[...].astype(F32)).astype(BF)
    out_ref[:, FF:] = (down_ref[...].astype(F32) + down_in_ref[...].astype(F32)).astype(BF)


def merge(core, d_up, d_down, up_in, down_in, rows):
    kept = pl.BlockSpec((rows, FF), lambda i, c: (2 * i + c[0], 0))
    came = pl.BlockSpec((rows, FF), lambda i, c: (i, 0))
    count = up_in.shape[0] // rows
    return pl.pallas_call(
        merge_kernel,
        grid_spec=pltpu.PrefetchScalarGridSpec(
            num_scalar_prefetch=1,
            grid=(count,),
            in_specs=[kept, kept, came, came],
            out_specs=pl.BlockSpec((rows, 2 * FF), lambda i, c: (i, 0)),
        ),
        out_shape=jax.ShapeDtypeStruct((count * rows, 2 * FF), BF),
        compiler_params=pltpu.CompilerParams(vmem_limit_bytes=32 * MIB),
        cost_estimate=pl.CostEstimate(flops=2 * D * FF, bytes_accessed=14 * MIB, transcendentals=0),
        name="merge",
    )(core, d_up, d_down, up_in, down_in)


def prepare_kernel(x_ref, g_ref, gain_ref, shift_ref, na_t_ref, nf_ref, nf_t_ref, g_t_ref):
    x = x_ref[...].astype(F32)
    centred = x - jnp.mean(x, axis=-1, keepdims=True)
    hat = centred * lax.rsqrt(jnp.mean(centred * centred, axis=-1, keepdims=True) + NORM_EPS)
    na_t_ref[...] = (hat * gain_ref[0:1, :] + shift_ref[0:1, :]).T.astype(BF)
    nf = hat * gain_ref[1:2, :] + shift_ref[1:2, :]
    nf_ref[...] = nf.astype(BF)
    nf_t_ref[...] = nf.T.astype(BF)
    g_t_ref[...] = g_ref[...].astype(F32).T.astype(BF)


def prepare(x, g, gains, shifts):
    block = 512
    rows = pl.BlockSpec((block, D), lambda i: (i, 0))
    cols = pl.BlockSpec((D, block), lambda i: (0, i))
    fixed = pl.BlockSpec((2, D), lambda i: (0, 0))
    turned = jax.ShapeDtypeStruct((D, TOK), BF)
    return pl.pallas_call(
        prepare_kernel,
        grid=(TOK // block,),
        in_specs=[rows, rows, fixed, fixed],
        out_specs=[cols, rows, cols, cols],
        out_shape=[turned, jax.ShapeDtypeStruct((TOK, D), BF), turned, turned],
        compiler_params=pltpu.CompilerParams(
            dimension_semantics=("arbitrary",), vmem_limit_bytes=48 * MIB
        ),
        cost_estimate=pl.CostEstimate(
            flops=20 * TOK * D, bytes_accessed=12 * TOK * D, transcendentals=TOK
        ),
        name="prepare",
    )(x, g, gains, shifts)


def grads_kernel(g_ref, mix_ref, gq_ref, gkv_ref, nt_ref, _, dqkv_ref, dout_ref, bsum_ref, qkv_acc, out_acc):
    i = pl.program_id(0)
    gq = gq_ref[...]
    gkv = gkv_ref[...]
    nt = nt_ref[...]

    @pl.when(i == 0)
    def _():
        qkv_acc[...] = jnp.zeros_like(qkv_acc)
        out_acc[...] = jnp.zeros_like(out_acc)
        bsum_ref[...] = jnp.zeros_like(bsum_ref)

    qkv_acc[:, 0:D] += dot_nt(nt, gq)
    qkv_acc[:, D:] += dot_nt(nt, gkv)
    out_acc[...] += dot(mix_ref[...], g_ref[...])
    ones = jnp.ones((8, gq.shape[1]), BF)
    bsum_ref[:, 0:D] += dot_nt(ones, gq)
    bsum_ref[:, D:] += dot_nt(ones, gkv)

    @pl.when(i == pl.num_programs(0) - 1)
    def _():
        dqkv_ref[...] = qkv_acc[...].astype(BF)
        dout_ref[...] = out_acc[...].astype(BF)


def grads(g, mix, gq, gkv, nt, after):
    block = 1024
    cols = pl.BlockSpec((D, block), lambda i: (0, i))

    def fixed(shape):
        return pl.BlockSpec(shape, lambda i: (0, 0))

    return pl.pallas_call(
        grads_kernel,
        grid=(TOK // block,),
        in_specs=[
            pl.BlockSpec((block, D), lambda i: (i, 0)), cols, cols,
            pl.BlockSpec((128, block), lambda i: (0, i)), cols, pl.BlockSpec(memory_space=pl.ANY),
        ],
        out_specs=[fixed((D, QKV)), fixed((D, D)), fixed((8, QKV))],
        scratch_shapes=[pltpu.VMEM((D, QKV), F32), pltpu.VMEM((D, D), F32)],
        out_shape=[
            jax.ShapeDtypeStruct((D, QKV), BF), jax.ShapeDtypeStruct((D, D), BF),
            jax.ShapeDtypeStruct((8, QKV), F32),
        ],
        compiler_params=pltpu.CompilerParams(
            dimension_semantics=("arbitrary",), vmem_limit_bytes=48 * MIB
        ),
        cost_estimate=pl.CostEstimate(
            flops=2 * TOK * D * (QKV + D), bytes_accessed=16 * MIB, transcendentals=0
        ),
        name="grads",
    )(g, mix, gq, gkv, nt, after)


def final_kernel(
    x_ref, g_ref, y_ref, df_ref, mix_ref, gq_ref, gkv_ref, wt_ref, wo_ref, gain_ref, bias_ref, _,
    out_ref, ig_ref, sums_ref,
):
    i = pl.program_id(0)
    x = x_ref[...].astype(F32)
    gf = g_ref[...].astype(F32)

    @pl.when(i == 0)
    def _():
        sums_ref[...] = jnp.zeros_like(sums_ref)

    da = dot_tn(gq_ref[...], wt_ref[0:D, :]) + dot_tn(gkv_ref[...], wt_ref[D:, :])
    out_ref[...] = (x + (dot_tn(mix_ref[...], wo_ref[...]) + y_ref[...] + bias_ref[...])).astype(BF)
    mean = jnp.mean(x, axis=-1, keepdims=True)
    centred = x - mean
    rstd = lax.rsqrt(jnp.mean(centred * centred, axis=-1, keepdims=True) + NORM_EPS)
    hat = centred * rstd
    df = df_ref[...]
    d_hat = da * gain_ref[0:1, :] + df * gain_ref[1:2, :]
    m1 = jnp.mean(d_hat, axis=-1, keepdims=True)
    m2 = jnp.mean(d_hat * hat, axis=-1, keepdims=True)
    ig_ref[...] = gf + rstd * (d_hat - m1 - hat * m2)
    for r, v in enumerate((da * hat, df * hat, da, df, gf)):
        sums_ref[r : r + 1, :] += jnp.sum(v, axis=0, keepdims=True)


def final(x, g, y, d_ffn, mix, gq, gkv, wt, wo, gains, bias, after):
    block = 512

    def rows(i):
        return (i, 0)

    def cols(i):
        return (0, i)

    def fixed(i):
        return (0, 0)

    return pl.pallas_call(
        final_kernel,
        grid=(TOK // block,),
        in_specs=[
            pl.BlockSpec((block, D), rows), pl.BlockSpec((block, D), rows),
            pl.BlockSpec((block, D), rows), pl.BlockSpec((block, D), rows),
            pl.BlockSpec((D, block), cols), pl.BlockSpec((D, block), cols),
            pl.BlockSpec((128, block), cols),
            pl.BlockSpec((QKV, D), fixed), pl.BlockSpec((D, D), fixed),
            pl.BlockSpec((2, D), fixed), pl.BlockSpec((1, D), fixed), pl.BlockSpec(memory_space=pl.ANY),
        ],
        out_specs=[
            pl.BlockSpec((block, D), rows), pl.BlockSpec((block, D), rows), pl.BlockSpec((8, D), fixed),
        ],
        out_shape=[
            jax.ShapeDtypeStruct((TOK, D), BF), jax.ShapeDtypeStruct((TOK, D), F32),
            jax.ShapeDtypeStruct((8, D), F32),
        ],
        compiler_params=pltpu.CompilerParams(
            dimension_semantics=("arbitrary",), vmem_limit_bytes=48 * MIB
        ),
        cost_estimate=pl.CostEstimate(
            flops=2 * TOK * D * (QKV + D), bytes_accessed=36 * MIB, transcendentals=TOK
        ),
        name="closing",
    )(x, g, y, d_ffn, mix, gq, gkv, wt, wo, gains, bias, after)


def eye_block(rows, n, row_lo):
    r = lax.broadcasted_iota(jnp.int32, (rows, n), 0) + row_lo
    return r == lax.broadcasted_iota(jnp.int32, (rows, n), 1)


def diagonal_sum(ref, n, blk):
    total = 0.0
    for r in range(0, n, blk):
        total += jnp.sum(jnp.where(eye_block(blk, blk, 0), ref[r : r + blk, r : r + blk], 0.0))
    return total


def shift_diagonal(ref, low_ref, level, n, blk):
    for r in range(0, n, blk):
        ref[r : r + blk, r : r + blk] -= jnp.where(eye_block(blk, blk, 0), level, 0.0)
        low_ref[r : r + blk, :] = ref[r : r + blk, :].astype(BF)


def recentre(ref, low_ref, n, blk):
    level = diagonal_sum(ref, n, blk) / n
    shift_diagonal(ref, low_ref, level, n, blk)
    return level


def gram_sweep(level, q0, n, blk, a, al, s, sl, t, tl, u, ul, first=False, last=False):
    p0 = NS_A + NS_B * level + NS_C * level * level
    s[...] = (NS_B + 2.0 * NS_C * level) * a[...] + NS_C * dot(al[...], al[...])
    sl[...] = s[...].astype(BF)
    if first:
        u[...] = s[...]
        q0 = p0
    else:
        u[...] = p0 * u[...] + q0 * s[...] + dot(sl[...], ul[...])
        q0 = p0 * q0
    q0 = q0 + recentre(u, ul, n, blk)
    if last:
        return level, q0
    t[...] = p0 * a[...] + level * s[...] + dot(sl[...], al[...])
    t0 = p0 * level + recentre(t, tl, n, blk)
    a[...] = p0 * t[...] + t0 * s[...] + dot(sl[...], tl[...])
    return p0 * t0 + recentre(a, al, n, blk), q0


def wide_kernel(down_ref, m_ref, u_ref, q_ref, a, al, s, sl, t, tl, u, ul):
    blk = 256

    @pl.when(down_ref[0] == 0)
    def _():
        a[...] = dot_nt(m_ref[...], m_ref[...])

    @pl.when(down_ref[0] != 0)
    def _():
        for q in range(4):
            part = m_ref[:, q * D : (q + 1) * D]
            if q == 0:
                a[...] = dot_tn(part, part)
            else:
                a[...] += dot_tn(part, part)

    inverse = 1.0 / (jnp.sqrt(jnp.full((1, D), diagonal_sum(a, D, blk))) + 1e-07)
    a[...] = a[...] * (inverse * inverse)
    level = recentre(a, al, D, blk)
    state = (a, al, s, sl, t, tl, u, ul)

    def sweep(k, carry):
        return gram_sweep(carry[0], carry[1], D, blk, *state)

    carry = gram_sweep(level, None, D, blk, *state, first=True)
    carry = lax.fori_loop(1, NS_STEPS - 1, sweep, carry)
    _, q0 = gram_sweep(carry[0], carry[1], D, blk, *state, last=True)
    u_ref[...] = (u[...] * inverse).astype(BF)
    q_ref[...] = q0 * inverse


def wide_ns(down, m):
    big, low = pltpu.VMEM((D, D), F32), pltpu.VMEM((D, D), BF)

    def fixed(i, d):
        return (0, 0)

    return pl.pallas_call(
        wide_kernel,
        grid_spec=pltpu.PrefetchScalarGridSpec(
            num_scalar_prefetch=1,
            grid=(1,),
            in_specs=[pl.BlockSpec((D, FF), lambda i, d: (0, d[0]), pipeline_mode=pl.Buffered(1))],
            out_specs=[pl.BlockSpec((D, D), fixed), pl.BlockSpec((1, D), fixed)],
            scratch_shapes=[big, low] * 4,
        ),
        out_shape=[jax.ShapeDtypeStruct((D, D), BF), jax.ShapeDtypeStruct((1, D), F32)],
        compiler_params=pltpu.CompilerParams(vmem_limit_bytes=48 * MIB),
        cost_estimate=pl.CostEstimate(flops=2 * 24 * D**3, bytes_accessed=6 * MIB, transcendentals=D),
        name="wide_ns",
    )(down, m)


def square_kernel(m_ref, kv_ref, o_ref, okv_ref, x, xl, a, al, sl, *small):
    blk = 256
    n = 2 * HEAD_DIM
    m = m_ref[...].astype(F32)
    x[...] = m / (jnp.sqrt(jnp.full((1, D), jnp.sum(m * m))) + 1e-07)
    sa, sal, ss, ssl, st, stl, su, sul = small
    kv = kv_ref[...]
    sa[...] = dot_tn(kv, kv)
    inverse = 1.0 / (jnp.sqrt(jnp.full((1, n), diagonal_sum(sa, n, n))) + 1e-07)
    sa[...] = sa[...] * (inverse * inverse)
    su[...] = jnp.zeros_like(su)
    sul[...] = jnp.zeros_like(sul)
    level = recentre(sa, sal, n, n)

    def sweep(k, carry):
        xl[...] = x[...].astype(BF)
        a[...] = dot_nt(xl[...], xl[...])
        lev = recentre(a, al, D, blk)
        p0 = NS_A + NS_B * lev + NS_C * lev * lev
        small_next = gram_sweep(carry[0], carry[1], n, n, sa, sal, ss, ssl, st, stl, su, sul)
        sl[...] = ((NS_B + 2.0 * NS_C * lev) * a[...] + NS_C * dot(al[...], al[...])).astype(BF)
        x[...] = p0 * x[...] + dot(sl[...], xl[...])
        return small_next

    _, q0 = lax.fori_loop(0, NS_STEPS, sweep, (level, jnp.float32(1.0)))
    o_ref[...] = x[...]
    okv_ref[...] = (q0 * kv.astype(F32) + dot(kv, sul[...])) * inverse


def square_ns(m, kv):
    big, low = pltpu.VMEM((D, D), F32), pltpu.VMEM((D, D), BF)
    n = 2 * HEAD_DIM
    return pl.pallas_call(
        square_kernel,
        in_specs=[pl.BlockSpec(memory_space=pltpu.VMEM)] * 2,
        out_specs=[pl.BlockSpec(memory_space=pltpu.VMEM)] * 2,
        scratch_shapes=[big, low, big, low, low]
        + [pltpu.VMEM((n, n), F32), pltpu.VMEM((n, n), BF)] * 4,
        out_shape=[jax.ShapeDtypeStruct((D, D), F32), jax.ShapeDtypeStruct((D, n), F32)],
        compiler_params=pltpu.CompilerParams(vmem_limit_bytes=48 * MIB),
        cost_estimate=pl.CostEstimate(flops=2 * 17 * D**3, bytes_accessed=6 * MIB, transcendentals=D),
        name="square_ns",
    )(m, kv)


def swap(x, axis, bit):
    return lax.ppermute(x, axis, [(i, i ^ bit) for i in range(lax.axis_size(axis))])


def bits_of(size):
    return [1 << b for b in range(size.bit_length() - 1)]


class Grid:
    def __init__(self):
        chip, narrow = bits_of(lax.axis_size("chip")), bits_of(lax.axis_size("narrow"))
        self.axes = [("chip", b) for b in reversed(chip)] + [("core", 1)]
        self.axes += [("narrow", b) for b in reversed(narrow)]
        self.chip = list(range(len(chip)))
        self.core = len(chip)
        self.narrow = list(range(len(chip) + 1, len(self.axes)))

    def bit(self, place):
        axis, bit = self.axes[place]
        return (lax.axis_index(axis) // bit) % 2

    def swap(self, x, place):
        return swap(x, *self.axes[place])

    def gather(self, x, order):
        x = x.reshape((1,) * len(self.axes) + x.shape)
        for place in order:
            other = self.swap(x, place)
            up = self.bit(place) == 1
            x = jnp.concatenate([jnp.where(up, other, x), jnp.where(up, x, other)], axis=place)
        return x.reshape((-1,) + x.shape[len(self.axes) + 1 :])

    def scatter(self, x, order):
        x = x.reshape((2,) * len(self.axes) + (-1,) + x.shape[1:])
        for place in order:
            bit = self.bit(place)
            away = lax.dynamic_index_in_dim(x, 1 - bit, place, keepdims=True).astype(BF)
            keep = lax.dynamic_index_in_dim(x, bit, place, keepdims=True).astype(F32)
            x = keep + self.swap(away, place).astype(F32)
        return x.reshape((-1,) + x.shape[len(self.axes) + 1 :])


def locate(lengths):
    ends = jnp.cumsum(lengths)
    token_ids = jnp.arange(TOK, dtype=jnp.int32)
    starts = jnp.max(jnp.where(ends[None, :] <= token_ids[:, None], ends[None, :], 0), axis=1)
    return starts, token_ids - starts


def up_columns(x):
    return x.reshape(x.shape[0], FF // FC, FC // 4, 4).swapaxes(2, 3).reshape(x.shape[0], FF)


def up_columns_back(x):
    return x.reshape(x.shape[0], FF // FC, 4, FC // 4).swapaxes(2, 3).reshape(x.shape[0], FF)


def per_device(
    block_input, doc_lengths, cotangent,
    weight_query, weight_keyval, weight_output, weight_expand, weight_reduce,
    momentum_query, momentum_keyval, momentum_output, momentum_expand, momentum_reduce,
    norm_gains, norm_biases, proj_biases, adam_first, adam_second,
):
    grid = Grid()
    chips, narrow = lax.axis_size("chip"), lax.axis_size("narrow")
    devices = 2 * chips * narrow
    core = lax.axis_index("core")
    place = lax.axis_index("chip") * narrow + lax.axis_index("narrow")
    masters = (weight_query, weight_keyval, weight_output, weight_expand, weight_reduce)
    own = D // devices
    up_first = grid.narrow[::-1] + grid.chip[::-1] + [grid.core]
    down_first = grid.narrow[::-1] + grid.chip + [grid.core]

    w_qkv = grid.gather(jnp.concatenate([weight_query, weight_keyval], axis=1).astype(BF), up_first)
    w_out = grid.gather(weight_output.astype(BF), down_first)
    ffn_pack = jnp.concatenate(
        [up_columns(weight_expand), weight_reduce.reshape(own, 4 * D)], axis=1
    ).astype(BF)
    ffn_weights = lax.all_gather(ffn_pack, ("chip", "core", "narrow"), axis=0, tiled=True)
    bias_qkv = proj_biases[:QKV]
    bias_output = proj_biases[QKV : QKV + D]
    bias_expand = proj_biases[QKV + D : QKV + D + FF]
    bias_reduce = proj_biases[QKV + D + FF :]

    n_attn_t, n_ffn, n_ffn_t, g_t = prepare(block_input, cotangent, norm_gains, norm_biases)

    starts, positions = locate(doc_lengths[0])
    frequency = ROPE_BASE ** (-(2.0 * jnp.arange(ROT // 2, dtype=F32)) / ROT)
    angles = positions.astype(F32)[None, :] * frequency[:, None]
    cos, sin = jnp.cos(angles), jnp.sin(angles)
    first_block = starts[::QB] // QB

    qkv_t = dot_tn(w_qkv, n_attn_t) + bias_qkv[:, None]
    grad_mixed_t = dot_nt(w_out, cotangent).astype(BF)
    so_far = attention(first_block, qkv_t, grad_mixed_t, cos, sin, cos, 0, 1, None)
    y, d_ffn, d_up, d_down, d_bias_up = ffn(
        n_ffn, n_ffn_t, cotangent, g_t, ffn_weights, up_columns(bias_expand[None, :]), so_far[0]
    )
    came = [
        swap(
            lax.dynamic_index_in_dim(d.reshape(chips, 2, narrow * own, FF), 1 - core, 1, keepdims=False),
            "core", 1,
        ).reshape(D // 2, FF)
        for d in (d_up, d_down)
    ]
    core_id = core.astype(jnp.int32).reshape(1)
    packed = merge(core_id, d_up, d_down, *came, narrow * own)
    ffn_grads = lax.psum_scatter(packed, "chip", scatter_dimension=0, tiled=True)
    mix_t, gq_t, _, gkv_t = attention(
        first_block, qkv_t, grad_mixed_t, cos, sin, packed, 1, HEADS // NH - 1, so_far
    )
    ffn_grads, _ = lax.optimization_barrier((ffn_grads, gkv_t))
    d_qkv, d_out, bias_sums = grads(cotangent, mix_t, gq_t, gkv_t, n_attn_t, ffn_grads)
    ffn_grads = lax.psum_scatter(ffn_grads, "narrow", scatter_dimension=0, tiled=True)
    scatter_up = [grid.core] + grid.chip + grid.narrow
    scatter_down = [grid.core] + grid.chip[::-1] + grid.narrow
    qkv_sum = grid.scatter(d_qkv, scatter_up)
    block_output, input_grad, sums = final(
        block_input, cotangent, y, d_ffn, mix_t, gq_t, gkv_t, w_qkv.T, w_out,
        norm_gains, (bias_output + bias_reduce)[None, :], bias_sums,
    )
    vector = jnp.concatenate(
        [sums[0], sums[1], sums[2], sums[3], bias_sums[0], sums[4], up_columns_back(d_bias_up)[0], sums[4]]
    )
    entries = vector.shape[0]
    share = -(-entries // devices)
    vector = jnp.pad(vector, (0, share * devices - entries)).reshape(devices, share)
    vector = jnp.pad(vector, ((0, 0), (0, own * 128 - share))).reshape(D, 128)
    out_sum = grid.scatter(jnp.concatenate([d_out, vector.astype(BF)], axis=1), scatter_down)

    ffn_grads = lax.optimization_barrier((ffn_grads, sums))[0].astype(F32)
    new_expand = MUON_MOMENTUM * momentum_expand + up_columns_back(ffn_grads[:, :FF])
    new_reduce = MUON_MOMENTUM * momentum_reduce + ffn_grads[:, FF:].reshape(-1, D)
    ffn_momenta = jnp.concatenate([new_expand, new_reduce.reshape(own, 4 * D)], axis=1).astype(BF)
    ffn_whole = lax.all_gather(ffn_momenta, ("chip", "core", "narrow"), axis=0, tiled=True)
    new_query = MUON_MOMENTUM * momentum_query + qkv_sum[:, :D]
    new_keyval = MUON_MOMENTUM * momentum_keyval + qkv_sum[:, D:QKV]
    new_output = MUON_MOMENTUM * momentum_output + out_sum[:, :D]

    def for_core(first, second):
        mine = jnp.where(core == 0, first, second)
        theirs = swap(jnp.where(core == 0, second, first), "core", 1)
        return jnp.concatenate(
            [jnp.where(core == 0, mine, theirs), jnp.where(core == 0, theirs, mine)], axis=0
        )

    rank = (lax.axis_index("chip") * 2 + core) * narrow + lax.axis_index("narrow")
    sibling = rank + (1 - 2 * core) * narrow

    def both_rows(m):
        return jnp.concatenate(
            [lax.dynamic_slice_in_dim(m, r * own, own, 0) for r in (rank, sibling)], axis=0
        )

    u, q0 = wide_ns(core_id, ffn_whole)
    rows_m = both_rows(ffn_whole)
    as_up = dot(both_rows(u), ffn_whole[:, :FF])
    as_down = jnp.concatenate(
        [dot(rows_m[:, FF + q * D : FF + (q + 1) * D], u) for q in range(4)], axis=1
    )
    rows_m = rows_m.astype(F32) * q0[0, 0]
    rows_o = jnp.where(core == 0, rows_m[:, :FF] + as_up, rows_m[:, FF:] + as_down)
    mine, theirs = rows_o[:own], swap(rows_o[own:], "core", 1)
    o_expand = jnp.where(core == 0, mine, theirs)
    o_reduce = jnp.where(core == 0, theirs, mine).reshape(-1, D)

    first_sum = out_sum[:, D:]
    high = first_sum.astype(BF)
    extra = jnp.concatenate(
        [new_keyval.astype(BF), high, (first_sum - high.astype(F32)).astype(BF)], axis=1
    )
    pair = for_core(
        jnp.concatenate([new_query.astype(BF), extra], axis=1),
        jnp.concatenate([new_output.astype(BF), extra], axis=1),
    )
    wide = 640
    whole = jnp.concatenate(
        [
            grid.gather(pair[:, :wide], grid.narrow[::-1] + grid.chip[::-1]),
            grid.gather(pair[:, wide:], grid.narrow[::-1] + grid.chip),
        ],
        axis=1,
    )
    o_pair, o_kv = square_ns(whole[:, :D], whole[:, D:QKV])
    row_lo = place * (2 * own)
    mine = lax.dynamic_slice_in_dim(o_pair, row_lo + core * own, own, 0)
    theirs = swap(lax.dynamic_slice_in_dim(o_pair, row_lo + (1 - core) * own, own, 0), "core", 1)
    o_query = jnp.where(core == 0, mine, theirs)
    o_output = jnp.where(core == 0, theirs, mine)
    o_keyval = lax.dynamic_slice_in_dim(o_kv, row_lo + core * own, own, 0)
    vector_grad = (
        whole[:, QKV : QKV + 128].astype(F32) + whole[:, QKV + 128 :].astype(F32)
    ).reshape(chips, narrow, 2, own * 128).swapaxes(1, 2).reshape(devices, own * 128)
    vector_grad = vector_grad[:, :share].reshape(-1)[:entries]

    new_momenta = (new_query, new_keyval, new_output, new_expand, new_reduce)
    new_weights = []
    for master, o in zip(masters, (o_query, o_keyval, o_output, o_expand, o_reduce)):
        factor = math.sqrt(max(1.0, master.shape[0] * devices / master.shape[1]))
        new_weights.append(master - MUON_RATE * factor * o)

    params = jnp.concatenate([norm_gains.reshape(-1), norm_biases.reshape(-1), proj_biases])
    vector_first = BETA_FIRST * adam_first + (1.0 - BETA_FIRST) * vector_grad
    vector_second = BETA_SECOND * adam_second + (1.0 - BETA_SECOND) * vector_grad * vector_grad
    corrected_first = vector_first / (1.0 - BETA_FIRST**STEP)
    corrected_second = vector_second / (1.0 - BETA_SECOND**STEP)
    vector_new = params - ADAM_RATE * corrected_first / (jnp.sqrt(corrected_second) + ADAM_EPS)
    return (
        block_output, input_grad, *new_momenta, *new_weights, vector_first, vector_second, vector_new
    )


def solution(mesh):
    wide, narrow = mesh.shape["wide"], mesh.shape["narrow"]
    grid = Mesh(mesh.devices.reshape(wide // 2, 2, narrow), ("chip", "core", "narrow"))
    rows = P(("chip", "core", "narrow"), None)
    in_specs = (rows,) * 13 + (P(),) * 5
    out_specs = (rows,) * 12 + (P(),) * 3
    return jax.shard_map(
        per_device, mesh=grid, in_specs=in_specs, out_specs=out_specs, check_vma=False
    )
```
